32 devices in a mesh: blk: 16 (over z, y, core), head: 2 (over x).
Axes of the slice: x: 2, y: 2, z: 4, core: 2. Of those that a mesh axis runs over, the one named last changes fastest.
Arguments:
- queries: bfloat16 [512, 3072], P(('blk', 'head')), may hold values from -8 to 8
- query_tangent: bfloat16 [512, 3072], P(('blk', 'head')), may hold values from -3 to 3
- key_rows: bfloat16 [2048, 3072], P(('blk', 'head')), may hold values from -8 to 8
- key_tangent: bfloat16 [2048, 3072], P(('blk', 'head')), may hold values from -3 to 3
- value_rows: bfloat16 [2048, 3072], P(('blk', 'head')), may hold values from -24 to 24
- value_tangent: bfloat16 [2048, 3072], P(('blk', 'head')), may hold values from -3 to 3
- out_weight: bfloat16 [3072, 5120], P('head'), may hold values from -0.109375 to 0.109375
Outputs:
- projected: bfloat16 [512, 5120], P('blk', 'head')
- projected_tangent: bfloat16 [512, 5120], P('blk', 'head')
The draws below stay inside these ranges and needn't reach their ends.
All inputs are finite; a program needn't handle non-finite values.
Results may differ from the reference program's by a relative error of at most 0.0107.
Values may be sent and summed in bfloat16 or wider, within the bound.
No kernel may reach another device: no remote copies, remote signals or barrier semaphores. Data moves between devices by JAX's collectives and lax.ppermute only.
A program may use at most 128 MiB of HBM per device.

```python
import jax
import jax.numpy as jnp
from jax import lax

D = 5120
H = 24
DH = 128
TOKENS = 2048
QTOK = 512


def draw_queries(key, part):
    key = jax.random.fold_in(key, 1)
    drawn = 1.4 * jax.random.truncated_normal(key, -5.0, 5.0, (QTOK, H * DH), jnp.float32)
    return jnp.clip(drawn, -8.0, 8.0).astype(jnp.bfloat16)


def draw_key_rows(key, part):
    key = jax.random.fold_in(key, 2)
    drawn = 1.4 * jax.random.truncated_normal(key, -5.0, 5.0, (TOKENS, H * DH), jnp.float32)
    return jnp.clip(drawn, -8.0, 8.0).astype(jnp.bfloat16)


def level_of(rng, extent, cuts, least, high):
    gain = 1.0
    for dim, shards_of in cuts:
        steps = jax.random.uniform(jax.random.fold_in(jax.random.fold_in(rng, 6), dim), (shards_of,), jnp.float32, least / len(cuts), high / len(cuts))
        gain = gain * jnp.repeat(jnp.exp(steps), extent[dim] // shards_of).reshape((-1,) + (1,) * (len(extent) - 1 - dim))
    return gain


def noise(stream_key, extent, scale, limit, shards=(), dtype=jnp.bfloat16):
    entries = jax.random.normal(stream_key, extent, jnp.float32) * scale
    if len(shards) > 0:
        entries = level_of(stream_key, extent, shards, -0.22, 0.18) * entries
    return jnp.clip(entries, min=-limit, max=limit).astype(dtype)


def setup_inputs(seed: int = 0) -> dict:
    splits = jax.random.split(jax.random.key(seed), 8)
    queries = draw_queries(jax.random.fold_in(splits[7], 71), 0)
    query_tangent = noise(splits[1], (QTOK, H * DH), 0.5, 3.0, ((0, 32),))
    key_rows = draw_key_rows(jax.random.fold_in(splits[7], 71), 0)
    key_tangent = noise(splits[3], (TOKENS, H * DH), 0.5, 3.0, ((0, 32),))
    value_rows = noise(splits[4], (TOKENS, H * DH), 4.0, 24.0, ((0, 32),))
    value_tangent = noise(splits[5], (TOKENS, H * DH), 0.5, 3.0, ((0, 32),))
    out_weight = noise(splits[6], (H * DH, D), (H * DH) ** -0.5, 0.109375, ((0, 2),))
    return dict(queries=queries, query_tangent=query_tangent, key_rows=key_rows, key_tangent=key_tangent, value_rows=value_rows, value_tangent=value_tangent, out_weight=out_weight)


def head_attention(head_parts):
    queries, query_tangent, key_rows, key_tangent, value_rows, value_tangent = head_parts
    score_scale = DH ** -0.5
    scores = jnp.dot(queries, key_rows.T, preferred_element_type=jnp.float32) * score_scale
    slopes = (jnp.dot(query_tangent, key_rows.T, preferred_element_type=jnp.float32)
              + jnp.dot(queries, key_tangent.T, preferred_element_type=jnp.float32)) * score_scale
    row_peak = jnp.max(scores, axis=1, keepdims=True)
    unnormed = jnp.exp(scores - row_peak)
    tilted_full = unnormed * slopes
    row_total = jnp.sum(unnormed, axis=1, keepdims=True)
    slope_sum = jnp.sum(tilted_full, axis=1, keepdims=True)
    weights = unnormed.astype(jnp.bfloat16)
    tilted = tilted_full.astype(jnp.bfloat16)
    value_sum = jnp.dot(weights, value_rows, preferred_element_type=jnp.float32)
    tangent_sum = (jnp.dot(tilted, value_rows, preferred_element_type=jnp.float32)
                   + jnp.dot(weights, value_tangent, preferred_element_type=jnp.float32))
    attended = value_sum / row_total
    attended_tangent = tangent_sum / row_total - (slope_sum / row_total) * attended
    return attended.astype(jnp.bfloat16), attended_tangent.astype(jnp.bfloat16)


def to_heads(matrix):
    return jnp.transpose(matrix.reshape(matrix.shape[0], H, DH), (1, 0, 2))


def from_heads(stacked):
    return jnp.transpose(stacked, (1, 0, 2)).reshape(stacked.shape[1], H * DH)


def reference(queries, query_tangent, key_rows, key_tangent, value_rows, value_tangent, out_weight):
    head_parts = tuple(to_heads(matrix) for matrix in (queries, query_tangent, key_rows, key_tangent, value_rows, value_tangent))
    attended, attended_tangent = lax.map(head_attention, head_parts)
    attended = from_heads(attended)
    attended_tangent = from_heads(attended_tangent)
    projected = jnp.dot(attended, out_weight, preferred_element_type=jnp.float32).astype(jnp.bfloat16)
    projected_tangent = jnp.dot(attended_tangent, out_weight, preferred_element_type=jnp.float32).astype(jnp.bfloat16)
    return projected, projected_tangent
```

```python
import functools
import math

import jax
import jax.numpy as jnp
from jax import lax
from jax.experimental import pallas as pl
from jax.experimental.pallas import tpu as pltpu
from jax.sharding import Mesh, PartitionSpec as P

H = 24
DH = 128
NT = (((1,), (1,)), ((), ()))
STATS = 5


def split_bf16(x, parts):
    terms = []
    for _ in range(parts):
        term = x.astype(jnp.bfloat16)
        terms.append(term)
        x = x - term.astype(jnp.float32)
    return terms


def attend_kernel(heads, planes_of, row_len, plane_ref, *refs):
    query_refs, (kv_ref, out_ref) = refs[:-2], refs[-2:]
    h = pl.program_id(0)
    group, _, key_rows, _ = kv_ref.shape
    keys = group * key_rows
    g_count, head_axis = out_ref.shape[1], out_ref.shape[2] // row_len
    key, key_tan, value, value_tan = (kv_ref[:, t].reshape(keys, DH) for t in range(4))
    key_pair = jnp.concatenate([key, key_tan], axis=1)
    value_pair = jnp.concatenate([value, value_tan], axis=1)
    scale = DH ** (-0.5)
    data = pl.ds(pl.multiple_of(h * 2 * DH, 2 * DH), 2 * DH)
    tail = pl.ds(heads * 2 * DH, DH)

    def one_plane(q_ref, j, plane):
        rows = group * row_len
        query = q_ref[j, :, 0].reshape(rows, DH)
        qtan = q_ref[j, :, 1].reshape(rows, DH)
        scores = lax.dot_general(query, key, NT, preferred_element_type=jnp.float32) * scale
        slopes = (
            lax.dot_general(
                jnp.concatenate([qtan, query], axis=1),
                key_pair,
                NT,
                preferred_element_type=jnp.float32,
            )
            * scale
        )
        peak = jnp.max(scores, axis=1, keepdims=True)
        unnormed = jnp.exp(scores - peak)
        tilted = unnormed * slopes
        total = jnp.sum(unnormed, axis=1, keepdims=True)
        slope_sum = jnp.sum(tilted, axis=1, keepdims=True)
        sums = jnp.dot(
            unnormed.astype(jnp.bfloat16), value_pair, preferred_element_type=jnp.float32
        )
        tilted_sum = jnp.dot(
            tilted.astype(jnp.bfloat16), value, preferred_element_type=jnp.float32
        )
        inv = 1.0 / total
        mean_slope = slope_sum * inv
        mean_value = sums[:, :DH] * inv
        tangent = (sums[:, DH:] + tilted_sum) * inv - mean_slope * mean_value
        both = jnp.concatenate([mean_value, tangent], axis=1).astype(jnp.bfloat16)
        lse = peak + jnp.log(total)
        stats = split_bf16(lse, 3) + split_bf16(mean_slope, 2)
        lane = lax.broadcasted_iota(jnp.int32, (rows, DH), 1)
        packed = jnp.zeros((rows, DH), jnp.float32)
        for i, stat in enumerate(stats):
            packed = jnp.where(lane == i * heads + h, stat.astype(jnp.float32), packed)
        for x in range(head_axis):
            for g in range(g_count):
                here = slice((x * g_count + g) * row_len, (x * g_count + g + 1) * row_len)
                there = pl.ds(x * row_len, row_len)
                out_ref[plane, g, there, data] = both[here]
                before = jnp.where(
                    h == 0, 0.0, out_ref[plane, g, there, tail].astype(jnp.float32)
                )
                out_ref[plane, g, there, tail] = (before + packed[here]).astype(jnp.bfloat16)

    for i, q_ref in enumerate(query_refs):
        count = q_ref.shape[0]
        if count == 1:
            one_plane(q_ref, 0, planes_of(plane_ref[0], i))
        else:
            pl.loop(0, count)(lambda j, q_ref=q_ref: one_plane(q_ref, j, j))


def attend(queries, kv, plane, planes_of, k, g_count, head_axis):
    group, _, key_rows, width = kv.shape
    heads = width // DH
    row_len = queries[0].shape[3]
    out_shape = (k, g_count, head_axis * row_len, heads * 2 * DH + DH)

    def by_head(*shape):
        return pl.BlockSpec(shape + (DH,), lambda h, _: (0,) * len(shape) + (h,))

    return pl.pallas_call(
        functools.partial(attend_kernel, heads, planes_of, row_len),
        out_shape=jax.ShapeDtypeStruct(out_shape, jnp.bfloat16),
        grid_spec=pltpu.PrefetchScalarGridSpec(
            num_scalar_prefetch=1,
            grid=(heads,),
            in_specs=[by_head(*q.shape[:-1]) for q in queries] + [by_head(*kv.shape[:-1])],
            out_specs=pl.BlockSpec(out_shape, lambda h, _: (0, 0, 0, 0)),
        ),
        compiler_params=pltpu.CompilerParams(vmem_limit_bytes=48 * 2**20),
        name="attend",
    )(plane, *queries, kv)


def merge(parts_ref, both_ref, heads):
    k, g_count, rows, _ = parts_ref.shape
    tail = heads * 2 * DH
    for g in range(g_count):
        stats = [parts_ref[j, g, :, tail : tail + DH].astype(jnp.float32) for j in range(k)]
        for h in range(heads):

            def stat(j, i):
                return stats[j][:, i * heads + h : i * heads + h + 1]

            lse = [stat(j, 0) + stat(j, 1) + stat(j, 2) for j in range(k)]
            slope = [stat(j, 3) + stat(j, 4) for j in range(k)]
            top = functools.reduce(jnp.maximum, lse)
            share = [jnp.exp(e - top) for e in lse]
            inv = 1.0 / sum(share)
            share = [e * inv for e in share]
            mean_slope = sum(e * s for e, s in zip(share, slope))
            value = jnp.zeros((rows, DH), jnp.float32)
            tangent = jnp.zeros((rows, DH), jnp.float32)
            for j in range(k):
                col = h * 2 * DH
                part = parts_ref[j, g, :, col : col + DH].astype(jnp.float32)
                part_tan = parts_ref[j, g, :, col + DH : col + 2 * DH].astype(jnp.float32)
                value += share[j] * part
                tangent += share[j] * part_tan + (share[j] * (slope[j] - mean_slope)) * part
            col = (g * heads + h) * DH
            both_ref[:rows, col : col + DH] = value.astype(jnp.bfloat16)
            both_ref[rows:, col : col + DH] = tangent.astype(jnp.bfloat16)


def first_kernel(heads, half_ref, parts_ref, weight_ref, out_ref, both_ref):
    @pl.when(pl.program_id(0) == 0)
    def _():
        merge(parts_ref, both_ref, heads)

    out_ref[...] = jnp.dot(
        both_ref[...], weight_ref[...], preferred_element_type=jnp.float32
    ).astype(out_ref.dtype)


def second_kernel(half_ref, both_ref, weight_ref, out_ref):
    out_ref[...] = jnp.dot(
        both_ref[...], weight_ref[...], preferred_element_type=jnp.float32
    ).astype(out_ref.dtype)


def project(kernel, half, left, weight, width, dtype, both, tile=512):
    depth = weight.shape[0]
    steps = width // tile
    fixed = pl.BlockSpec(left.shape, lambda n, s: (0,) * left.ndim)
    column = pl.BlockSpec((depth, tile), lambda n, s: (0, s[0] * steps + n))
    rows = both[0]
    outs = [jax.ShapeDtypeStruct((rows, width), dtype)]
    out_specs = [pl.BlockSpec((rows, tile), lambda n, s: (0, n))]
    if left.ndim > 2:
        outs.append(jax.ShapeDtypeStruct(both, jnp.bfloat16))
        out_specs.append(pl.BlockSpec(both, lambda n, s: (0, 0)))
    return pl.pallas_call(
        kernel,
        out_shape=outs,
        grid_spec=pltpu.PrefetchScalarGridSpec(
            num_scalar_prefetch=1,
            grid=(steps,),
            in_specs=[fixed, column],
            out_specs=out_specs,
        ),
        compiler_params=pltpu.CompilerParams(vmem_limit_bytes=48 * 2**20),
        cost_estimate=pl.CostEstimate(
            flops=2 * rows * depth * width, bytes_accessed=2 * depth * width, transcendentals=0
        ),
        name="project",
    )(half, left, weight)


def pack(group, *matrices):
    stacked = jnp.stack(matrices)
    count, rows, columns = stacked.shape
    return stacked.reshape(count, rows, group, columns // group).transpose(2, 0, 1, 3)


def local(queries, query_tangent, key_rows, key_tangent, value_rows, value_tangent, out_weight):
    k, g_count, head_axis = (lax.axis_size(a) for a in ("k", "g", "head"))
    plane_axes = ("head", "g")
    group = g_count * head_axis
    heads = H // group
    rows = queries.shape[0] * head_axis

    def within_plane(x):
        return lax.all_to_all(x, plane_axes, split_axis=0, concat_axis=0, tiled=True)

    plane_queries = within_plane(pack(group, queries, query_tangent))
    kv = within_plane(pack(group, key_rows, key_tangent, value_rows, value_tangent))
    if k in (2, 4, 8):
        all_queries = [plane_queries[None]] + [
            lax.ppermute(plane_queries, "k", [(i, i ^ d) for i in range(k)])[None]
            for d in range(1, k)
        ]
    else:
        all_queries = [lax.all_gather(plane_queries, "k", axis=0, tiled=False)]

    plane = lax.axis_index("k").astype(jnp.int32).reshape(1)
    parts = attend(all_queries, kv, plane, lambda z, d: z ^ d, k, g_count, head_axis)
    parts = parts.reshape((k * g_count,) + parts.shape[2:])
    parts = lax.all_to_all(parts, ("k", "g"), split_axis=0, concat_axis=0, tiled=True)
    parts = parts.reshape((k, g_count) + parts.shape[1:])

    width = out_weight.shape[1] // head_axis
    both_shape = (2 * rows, out_weight.shape[0])
    mine = lax.axis_index("head").astype(jnp.int32).reshape(1)
    merging = functools.partial(first_kernel, heads)
    if head_axis == 2:
        sent, both = project(
            merging, 1 - mine, parts, out_weight, width, jnp.bfloat16, both_shape
        )
        received = lax.ppermute(sent, "head", [(0, 1), (1, 0)])
        (own,) = project(
            second_kernel, mine, both, out_weight, width, jnp.float32, both_shape
        )
        total = own + received.astype(jnp.float32)
    else:
        partial, _ = project(
            merging, 0 * mine, parts, out_weight, width * head_axis, jnp.float32, both_shape
        )
        total = lax.psum_scatter(partial, "head", scatter_dimension=1, tiled=True)
    total = total.astype(jnp.bfloat16)
    return (total[:rows], total[rows:])


def solution(mesh):
    blk, head_axis = mesh.shape["blk"], mesh.shape["head"]
    g_count = math.gcd(H // head_axis, blk)
    fine = Mesh(mesh.devices.reshape(blk // g_count, g_count, head_axis), ("k", "g", "head"))
    rows = P(("k", "g", "head"), None)
    return jax.shard_map(
        local,
        mesh=fine,
        in_specs=(rows,) * 6 + (P("head", None),),
        out_specs=(P(("k", "g"), "head"),) * 2,
        check_vma=False,
    )
```

```python
import functools
import math

import jax
import jax.numpy as jnp
from jax import lax
from jax.experimental import pallas as pl
from jax.experimental.pallas import tpu as pltpu
from jax.sharding import Mesh, PartitionSpec as P

H = 24
DH = 128
NT = (((1,), (1,)), ((), ()))
ATTEND_VMEM = 24 * 2**20
PROJECT_VMEM = 20 * 2**20


def split_bf16(x, parts):
    terms = []
    for _ in range(parts):
        term = x.astype(jnp.bfloat16)
        terms.append(term)
        x = x - term.astype(jnp.float32)
    return terms


def attend_kernel(heads, row_len, plane_ref, *refs):
    query_refs, (kv_ref, out_ref) = refs[:-2], refs[-2:]
    group, _, key_rows, _ = kv_ref.shape
    keys = group * key_rows
    plane_rows = group * row_len
    g_count, head_axis = out_ref.shape[1], out_ref.shape[2] // row_len
    scale = DH ** (-0.5)

    def some_planes(blocks, planes):
        rows = len(blocks) * plane_rows
        lane = lax.broadcasted_iota(jnp.int32, (rows, DH), 1)
        packed = jnp.zeros((rows, DH), jnp.float32)

        def put(x, columns):
            for i, plane in enumerate(planes):
                for head in range(head_axis):
                    for g in range(g_count):
                        here = i * plane_rows + (head * g_count + g) * row_len
                        there = slice(head * row_len, (head + 1) * row_len)
                        out_ref[plane, g, there, columns] = x[here : here + row_len]

        for h in range(heads):
            lanes = slice(h * DH, (h + 1) * DH)
            key, key_tan, value, value_tan = (
                kv_ref[:, t, :, lanes].reshape(keys, DH) for t in range(4)
            )
            query, qtan = (
                jnp.concatenate(
                    [ref[j, :, t, :, lanes].reshape(plane_rows, DH) for ref, j in blocks]
                )
                for t in range(2)
            )
            scores = lax.dot_general(query, key, NT, preferred_element_type=jnp.float32) * scale
            slopes = (
                lax.dot_general(
                    jnp.concatenate([qtan, query], axis=1),
                    jnp.concatenate([key, key_tan], axis=1),
                    NT,
                    preferred_element_type=jnp.float32,
                )
                * scale
            )
            peak = jnp.max(scores, axis=1, keepdims=True)
            unnormed = jnp.exp(scores - peak)
            tilted = unnormed * slopes
            total = jnp.sum(unnormed, axis=1, keepdims=True)
            slope_sum = jnp.sum(tilted, axis=1, keepdims=True)
            sums = jnp.dot(
                unnormed.astype(jnp.bfloat16),
                jnp.concatenate([value, value_tan], axis=1),
                preferred_element_type=jnp.float32,
            )
            tilted_sum = jnp.dot(
                tilted.astype(jnp.bfloat16), value, preferred_element_type=jnp.float32
            )
            inv = 1.0 / total
            mean_slope = slope_sum * inv
            mean_value = sums[:, :DH] * inv
            tangent = (sums[:, DH:] + tilted_sum) * inv - mean_slope * mean_value
            both = jnp.concatenate([mean_value, tangent], axis=1).astype(jnp.bfloat16)
            put(both, slice(2 * h * DH, 2 * (h + 1) * DH))
            lse = peak + jnp.log(total)
            for i, stat in enumerate(split_bf16(lse, 3) + split_bf16(mean_slope, 2)):
                packed = jnp.where(lane == i * heads + h, stat.astype(jnp.float32), packed)
        put(packed.astype(jnp.bfloat16), slice(2 * heads * DH, (2 * heads + 1) * DH))

    if len(query_refs) > 1:
        planes = [plane_ref[0] ^ d for d in range(len(query_refs))]
        some_planes([(ref, 0) for ref in query_refs], planes)
    else:
        (ref,) = query_refs
        count = math.gcd(ref.shape[0], 4)

        @pl.loop(0, ref.shape[0] // count)
        def _(step):
            planes = [step * count + j for j in range(count)]
            some_planes([(ref, j) for j in planes], planes)


def attend(queries, kv, plane, k, g_count, head_axis):
    heads = kv.shape[3] // DH
    row_len = queries[0].shape[3]
    out_shape = (k, g_count, head_axis * row_len, heads * 2 * DH + DH)
    whole = pl.BlockSpec(memory_space=pltpu.VMEM)
    return pl.pallas_call(
        functools.partial(attend_kernel, heads, row_len),
        out_shape=jax.ShapeDtypeStruct(out_shape, jnp.bfloat16),
        in_specs=[pl.BlockSpec(memory_space=pltpu.SMEM)] + [whole] * (len(queries) + 1),
        out_specs=whole,
        compiler_params=pltpu.CompilerParams(vmem_limit_bytes=ATTEND_VMEM),
        name="attend",
    )(plane, *queries, kv)


def merge(parts_ref, both_ref, heads):
    k, g_count, rows, _ = parts_ref.shape
    tail = heads * 2 * DH
    for g in range(g_count):
        stats = [parts_ref[j, g, :, tail : tail + DH].astype(jnp.float32) for j in range(k)]
        for h in range(heads):

            def stat(j, i):
                return stats[j][:, i * heads + h : i * heads + h + 1]

            lse = [stat(j, 0) + stat(j, 1) + stat(j, 2) for j in range(k)]
            slope = [stat(j, 3) + stat(j, 4) for j in range(k)]
            top = functools.reduce(jnp.maximum, lse)
            share = [jnp.exp(e - top) for e in lse]
            inv = 1.0 / sum(share)
            share = [e * inv for e in share]
            mean_slope = sum(e * s for e, s in zip(share, slope))
            value = jnp.zeros((rows, DH), jnp.float32)
            tangent = jnp.zeros((rows, DH), jnp.float32)
            for j in range(k):
                col = h * 2 * DH
                part = parts_ref[j, g, :, col : col + DH].astype(jnp.float32)
                part_tan = parts_ref[j, g, :, col + DH : col + 2 * DH].astype(jnp.float32)
                value += share[j] * part
                tangent += share[j] * part_tan + (share[j] * (slope[j] - mean_slope)) * part
            col = (g * heads + h) * DH
            both_ref[:rows, col : col + DH] = value.astype(jnp.bfloat16)
            both_ref[rows:, col : col + DH] = tangent.astype(jnp.bfloat16)


def first_kernel(heads, half_ref, parts_ref, weight_ref, out_ref, both_ref, held, sems):
    copies = fetch(half_ref, weight_ref, held, sems)
    merge(parts_ref, both_ref, heads)
    times_held(copies, both_ref, out_ref, held)


def second_kernel(half_ref, both_ref, weight_ref, out_ref, held, sems):
    times_held(fetch(half_ref, weight_ref, held, sems), both_ref, out_ref, held)


def fetch(half_ref, weight_ref, held, sems):
    chunks, _, tile = held.shape
    copies = []
    for i in range(chunks):
        first = pl.multiple_of((half_ref[0] * chunks + i) * tile, tile)
        copy = pltpu.make_async_copy(weight_ref.at[:, pl.ds(first, tile)], held.at[i], sems.at[i])
        copy.start()
        copies.append(copy)
    return copies


def times_held(copies, both_ref, out_ref, held):
    tile = held.shape[2]
    for i, copy in enumerate(copies):
        copy.wait()
        out_ref[:, i * tile : (i + 1) * tile] = jnp.dot(
            both_ref[...], held[i], preferred_element_type=jnp.float32
        ).astype(out_ref.dtype)


def project(kernel, half, left, weight, width, dtype, merged=None):
    depth = weight.shape[0]
    chunks = 4
    rows = merged[0] if merged else left.shape[0]
    outs = [jax.ShapeDtypeStruct((rows, width), dtype)]
    if merged:
        outs.append(jax.ShapeDtypeStruct(merged, jnp.bfloat16))
    whole = pl.BlockSpec(memory_space=pltpu.VMEM)
    return pl.pallas_call(
        kernel,
        out_shape=outs,
        in_specs=[
            pl.BlockSpec(memory_space=pltpu.SMEM),
            whole,
            pl.BlockSpec(memory_space=pl.ANY),
        ],
        out_specs=[whole] * len(outs),
        scratch_shapes=[
            pltpu.VMEM((chunks, depth, width // chunks), jnp.bfloat16),
            pltpu.SemaphoreType.DMA((chunks,)),
        ],
        compiler_params=pltpu.CompilerParams(vmem_limit_bytes=PROJECT_VMEM),
        cost_estimate=pl.CostEstimate(
            flops=2 * rows * depth * width, bytes_accessed=2 * depth * width, transcendentals=0
        ),
        name="project",
    )(half, left, pltpu.with_memory_space_constraint(weight, pltpu.HBM))


def pack_kernel(*refs):
    *matrix_refs, out_ref, sems = refs
    group, _, _, width = out_ref.shape
    copies = [
        pltpu.make_async_copy(
            ref.at[:, pl.ds(i * width, width)], out_ref.at[i, t], sems.at[i, t]
        )
        for i in range(group)
        for t, ref in enumerate(matrix_refs)
    ]
    for copy in copies:
        copy.start()
    for copy in copies:
        copy.wait()


def pack(group, *matrices):
    rows, columns = matrices[0].shape
    return pl.pallas_call(
        pack_kernel,
        out_shape=jax.ShapeDtypeStruct(
            (group, len(matrices), rows, columns // group), jnp.bfloat16
        ),
        in_specs=[pl.BlockSpec(memory_space=pl.ANY)] * len(matrices),
        out_specs=pl.BlockSpec(memory_space=pltpu.VMEM),
        scratch_shapes=[pltpu.SemaphoreType.DMA((group, len(matrices)))],
        compiler_params=pltpu.CompilerParams(vmem_limit_bytes=8 * 2**20),
        name="pack",
    )(*(pltpu.with_memory_space_constraint(m, pltpu.HBM) for m in matrices))


def local(queries, query_tangent, key_rows, key_tangent, value_rows, value_tangent, out_weight):
    k, g_count, head_axis = (lax.axis_size(a) for a in ("k", "g", "head"))
    plane_axes = ("head", "g")
    group = g_count * head_axis
    heads = H // group
    rows = queries.shape[0] * head_axis

    def within_plane(x):
        return lax.all_to_all(x, plane_axes, split_axis=0, concat_axis=0, tiled=True)

    plane_queries = within_plane(pack(group, queries, query_tangent))
    kv = within_plane(pack(group, key_rows, key_tangent, value_rows, value_tangent))
    if k in (2, 4, 8):
        all_queries = [plane_queries[None]] + [
            lax.ppermute(plane_queries, "k", [(i, i ^ d) for i in range(k)])[None]
            for d in range(1, k)
        ]
    else:
        all_queries = [lax.all_gather(plane_queries, "k", axis=0, tiled=False)]

    plane = lax.axis_index("k").astype(jnp.int32).reshape(1)
    parts = attend(all_queries, kv, plane, k, g_count, head_axis)
    parts = parts.reshape((k * g_count,) + parts.shape[2:])
    parts = lax.all_to_all(parts, ("k", "g"), split_axis=0, concat_axis=0, tiled=True)
    parts = parts.reshape((k, g_count) + parts.shape[1:])

    width = out_weight.shape[1] // head_axis
    mine = lax.axis_index("head").astype(jnp.int32).reshape(1)
    merged = (2 * rows, out_weight.shape[0])
    merging = functools.partial(first_kernel, heads)
    if head_axis == 2:
        sent, both = project(merging, 1 - mine, parts, out_weight, width, jnp.bfloat16, merged)
        received = lax.ppermute(sent, "head", [(0, 1), (1, 0)])
        (own,) = project(second_kernel, mine, both, out_weight, width, jnp.float32)
        total = own + received.astype(jnp.float32)
    else:
        partial, _ = project(
            merging, 0 * mine, parts, out_weight, width * head_axis, jnp.float32, merged
        )
        total = lax.psum_scatter(partial, "head", scatter_dimension=1, tiled=True)
    total = total.astype(jnp.bfloat16)
    return (total[:rows], total[rows:])


def solution(mesh):
    blk, head_axis = mesh.shape["blk"], mesh.shape["head"]
    g_count = math.gcd(H // head_axis, blk)
    fine = Mesh(mesh.devices.reshape(blk // g_count, g_count, head_axis), ("k", "g", "head"))
    rows = P(("k", "g", "head"), None)
    return jax.shard_map(
        local,
        mesh=fine,
        in_specs=(rows,) * 6 + (P("head", None),),
        out_specs=(P(("k", "g"), "head"),) * 2,
        check_vma=False,
    )
```

```python
import functools
import math

import jax
import jax.numpy as jnp
from jax import lax
from jax.experimental import pallas as pl
from jax.experimental.pallas import tpu as pltpu
from jax.sharding import Mesh, PartitionSpec as P

H = 24
DH = 128
NT = (((1,), (1,)), ((), ()))
ATTEND_VMEM = 24 * 2**20
PROJECT_VMEM = 20 * 2**20


def split_bf16(x, parts):
    terms = []
    for _ in range(parts):
        term = x.astype(jnp.bfloat16)
        terms.append(term)
        x = x - term.astype(jnp.float32)
    return terms


def attend_kernel(heads, row_len, group, plane_ref, *refs):
    query_refs, kv_refs, out_ref = refs[: -group - 1], refs[-group - 1 : -1], refs[-1]
    plane_rows = group * row_len
    g_count, head_axis = out_ref.shape[1], out_ref.shape[2] // row_len
    scale = DH ** (-0.5)

    def some_planes(blocks, planes):
        rows = len(blocks) * plane_rows
        packed = jnp.zeros((rows, DH), jnp.float32)

        def put(x, columns):
            for i, plane in enumerate(planes):
                for head in range(head_axis):
                    for g in range(g_count):
                        here = i * plane_rows + (head * g_count + g) * row_len
                        there = slice(head * row_len, (head + 1) * row_len)
                        out_ref[plane, g, there, columns] = x[here : here + row_len]

        for h in range(heads):
            lanes = slice(h * DH, (h + 1) * DH)
            key, key_tan, value, value_tan = (
                jnp.concatenate([ref[t, :, lanes] for ref in kv_refs]) for t in range(4)
            )
            query, qtan = (
                jnp.concatenate(
                    [ref[j, :, t, :, lanes].reshape(plane_rows, DH) for ref, j in blocks]
                )
                for t in range(2)
            )
            scores = lax.dot_general(query, key, NT, preferred_element_type=jnp.float32) * scale
            slopes = (
                lax.dot_general(
                    jnp.concatenate([qtan, query], axis=1),
                    jnp.concatenate([key, key_tan], axis=1),
                    NT,
                    preferred_element_type=jnp.float32,
                )
                * scale
            )
            peak = jnp.max(scores, axis=1, keepdims=True)
            unnormed = jnp.exp(scores - peak)
            tilted = unnormed * slopes
            total = jnp.sum(unnormed, axis=1, keepdims=True)
            slope_sum = jnp.sum(tilted, axis=1, keepdims=True)
            sums = jnp.dot(
                unnormed.astype(jnp.bfloat16),
                jnp.concatenate([value, value_tan], axis=1),
                preferred_element_type=jnp.float32,
            )
            tilted_sum = jnp.dot(
                tilted.astype(jnp.bfloat16), value, preferred_element_type=jnp.float32
            )
            inv = 1.0 / total
            mean_slope = slope_sum * inv
            mean_value = sums[:, :DH] * inv
            tangent = (sums[:, DH:] + tilted_sum) * inv - mean_slope * mean_value
            both = jnp.concatenate([mean_value, tangent], axis=1).astype(jnp.bfloat16)
            put(both, slice(2 * h * DH, 2 * (h + 1) * DH))
            lse = peak + jnp.log(total)
            packed = stats_columns(packed, h, heads, lse, mean_slope)
        put(packed.astype(jnp.bfloat16), slice(2 * heads * DH, (2 * heads + 1) * DH))

    if len(query_refs) > 1:
        planes = [plane_ref[0] ^ d for d in range(len(query_refs))]
        some_planes([(ref, 0) for ref in query_refs], planes)
    else:
        (ref,) = query_refs
        count = math.gcd(ref.shape[0], 4)

        @pl.loop(0, ref.shape[0] // count)
        def _(step):
            planes = [step * count + j for j in range(count)]
            some_planes([(ref, j) for j in planes], planes)


def attend(queries, kv, plane, k, g_count, head_axis):
    heads = kv[0].shape[2] // DH
    row_len = queries[0].shape[3]
    out_shape = (k, g_count, head_axis * row_len, heads * 2 * DH + DH)
    whole = pl.BlockSpec(memory_space=pltpu.VMEM)
    return pl.pallas_call(
        functools.partial(attend_kernel, heads, row_len, len(kv)),
        out_shape=jax.ShapeDtypeStruct(out_shape, jnp.bfloat16),
        in_specs=[pl.BlockSpec(memory_space=pltpu.SMEM)] + [whole] * (len(queries) + len(kv)),
        out_specs=whole,
        compiler_params=pltpu.CompilerParams(vmem_limit_bytes=ATTEND_VMEM),
        name="attend",
    )(plane, *queries, *kv)


def merge_head(parts, stats, h, heads):
    def stat(j, i):
        return stats[j][:, i * heads + h : i * heads + h + 1]

    lse = [stat(j, 0) + stat(j, 1) + stat(j, 2) for j in range(len(parts))]
    slope = [stat(j, 3) + stat(j, 4) for j in range(len(parts))]
    top = functools.reduce(jnp.maximum, lse)
    share = [jnp.exp(e - top) for e in lse]
    total = sum(share)
    inv = 1.0 / total
    share = [e * inv for e in share]
    mean_slope = sum(e * s for e, s in zip(share, slope))
    value = tangent = 0.0
    for part, e, s in zip(parts, share, slope):
        col = h * 2 * DH
        own = part[:, col : col + DH].astype(jnp.float32)
        own_tan = part[:, col + DH : col + 2 * DH].astype(jnp.float32)
        value += e * own
        tangent += e * own_tan + (e * (s - mean_slope)) * own
    return value, tangent, top + jnp.log(total), mean_slope


def merge(parts_ref, both_ref, heads):
    k, g_count, rows, _ = parts_ref.shape
    tail = slice(2 * heads * DH, (2 * heads + 1) * DH)
    for g in range(g_count):
        parts = [parts_ref[j, g] for j in range(k)]
        stats = [part[:, tail].astype(jnp.float32) for part in parts]
        for h in range(heads):
            value, tangent, _, _ = merge_head(parts, stats, h, heads)
            col = (g * heads + h) * DH
            both_ref[:rows, col : col + DH] = value.astype(jnp.bfloat16)
            both_ref[rows:, col : col + DH] = tangent.astype(jnp.bfloat16)


def stats_columns(packed, h, heads, lse, slope):
    lane = lax.broadcasted_iota(jnp.int32, packed.shape, 1)
    for i, stat in enumerate(split_bf16(lse, 3) + split_bf16(slope, 2)):
        packed = jnp.where(lane == i * heads + h, stat.astype(jnp.float32), packed)
    return packed


def pair_kernel(heads, home_ref, away_ref, out_ref):
    rows = home_ref.shape[1]
    count = math.gcd(home_ref.shape[0], 8)

    @pl.loop(0, home_ref.shape[0] // count)
    def _(step):
        some = pl.ds(step * count, count)
        parts = [ref[some].reshape(count * rows, ref.shape[2]) for ref in (home_ref, away_ref)]
        tail = slice(2 * heads * DH, (2 * heads + 1) * DH)
        stats = [part[:, tail].astype(jnp.float32) for part in parts]
        packed = jnp.zeros((count * rows, DH), jnp.float32)

        def put(x, columns):
            out_ref[some, :, columns] = x.astype(jnp.bfloat16).reshape(count, rows, x.shape[1])

        for h in range(heads):
            value, tangent, lse, slope = merge_head(parts, stats, h, heads)
            put(jnp.concatenate([value, tangent], axis=1), slice(2 * h * DH, 2 * (h + 1) * DH))
            packed = stats_columns(packed, h, heads, lse, slope)
        put(packed, tail)


def merge_pair(home, away, heads):
    whole = pl.BlockSpec(memory_space=pltpu.VMEM)
    return pl.pallas_call(
        functools.partial(pair_kernel, heads),
        out_shape=jax.ShapeDtypeStruct(home.shape, home.dtype),
        in_specs=[whole, whole],
        out_specs=whole,
        compiler_params=pltpu.CompilerParams(vmem_limit_bytes=ATTEND_VMEM),
        name="merge_pair",
    )(home, away)


def first_kernel(heads, half_ref, parts_ref, weight_ref, out_ref, both_ref, held, sems):
    copies = fetch(half_ref, weight_ref, held, sems)
    merge(parts_ref, both_ref, heads)
    times_held(copies, both_ref, out_ref, held)


def second_kernel(half_ref, both_ref, weight_ref, out_ref, held, sems):
    times_held(fetch(half_ref, weight_ref, held, sems), both_ref, out_ref, held)


def fetch(half_ref, weight_ref, held, sems):
    chunks, _, tile = held.shape
    copies = []
    for i in range(chunks):
        first = pl.multiple_of((half_ref[0] * chunks + i) * tile, tile)
        copy = pltpu.make_async_copy(weight_ref.at[:, pl.ds(first, tile)], held.at[i], sems.at[i])
        copy.start()
        copies.append(copy)
    return copies


def times_held(copies, both_ref, out_ref, held):
    tile = held.shape[2]
    for i, copy in enumerate(copies):
        copy.wait()
        out_ref[:, i * tile : (i + 1) * tile] = jnp.dot(
            both_ref[...], held[i], preferred_element_type=jnp.float32
        ).astype(out_ref.dtype)


def project(kernel, half, left, weight, width, dtype, merged=None):
    depth = weight.shape[0]
    chunks = 4
    rows = merged[0] if merged else left.shape[0]
    outs = [jax.ShapeDtypeStruct((rows, width), dtype)]
    if merged:
        outs.append(jax.ShapeDtypeStruct(merged, jnp.bfloat16))
    whole = pl.BlockSpec(memory_space=pltpu.VMEM)
    return pl.pallas_call(
        kernel,
        out_shape=outs,
        in_specs=[
            pl.BlockSpec(memory_space=pltpu.SMEM),
            whole,
            pl.BlockSpec(memory_space=pl.ANY),
        ],
        out_specs=[whole] * len(outs),
        scratch_shapes=[
            pltpu.VMEM((chunks, depth, width // chunks), jnp.bfloat16),
            pltpu.SemaphoreType.DMA((chunks,)),
        ],
        compiler_params=pltpu.CompilerParams(vmem_limit_bytes=PROJECT_VMEM),
        cost_estimate=pl.CostEstimate(
            flops=2 * rows * depth * width, bytes_accessed=2 * depth * width, transcendentals=0
        ),
        name="project",
    )(half, left, pltpu.with_memory_space_constraint(weight, pltpu.HBM))


def pack_kernel(*refs):
    *matrix_refs, out_ref, sems = refs
    group, _, _, width = out_ref.shape
    copies = [
        pltpu.make_async_copy(
            ref.at[:, pl.ds(i * width, width)], out_ref.at[i, t], sems.at[i, t]
        )
        for i in range(group)
        for t, ref in enumerate(matrix_refs)
    ]
    for copy in copies:
        copy.start()
    for copy in copies:
        copy.wait()


def pack(group, *matrices):
    rows, columns = matrices[0].shape
    return pl.pallas_call(
        pack_kernel,
        out_shape=jax.ShapeDtypeStruct(
            (group, len(matrices), rows, columns // group), jnp.bfloat16
        ),
        in_specs=[pl.BlockSpec(memory_space=pl.ANY)] * len(matrices),
        out_specs=pl.BlockSpec(memory_space=pltpu.VMEM),
        scratch_shapes=[pltpu.SemaphoreType.DMA((group, len(matrices)))],
        compiler_params=pltpu.CompilerParams(vmem_limit_bytes=8 * 2**20),
        name="pack",
    )(*(pltpu.with_memory_space_constraint(m, pltpu.HBM) for m in matrices))


def pieces_kernel(group, columns_ref, after_ref, *refs):
    matrix_refs, out_refs, sems = refs[: -group - 1], refs[-group - 1 : -1], refs[-1]
    width = out_refs[0].shape[2]
    copies = []
    for d, out_ref in enumerate(out_refs):
        first = pl.multiple_of(columns_ref[d] * width, width)
        for t, ref in enumerate(matrix_refs):
            copies.append(
                pltpu.make_async_copy(ref.at[:, pl.ds(first, width)], out_ref.at[t], sems.at[d, t])
            )
    for copy in copies:
        copy.start()
    for copy in copies:
        copy.wait()


def pieces(group, order, after, *matrices):
    rows, columns = matrices[0].shape
    shape = jax.ShapeDtypeStruct((len(matrices), rows, columns // group), jnp.bfloat16)
    return pl.pallas_call(
        functools.partial(pieces_kernel, group),
        out_shape=[shape] * group,
        in_specs=[pl.BlockSpec(memory_space=pltpu.SMEM)]
        + [pl.BlockSpec(memory_space=pl.ANY)] * (1 + len(matrices)),
        out_specs=[pl.BlockSpec(memory_space=pltpu.VMEM)] * group,
        scratch_shapes=[pltpu.SemaphoreType.DMA((group, len(matrices)))],
        compiler_params=pltpu.CompilerParams(vmem_limit_bytes=8 * 2**20),
        name="pieces",
    )(order, after, *(pltpu.with_memory_space_constraint(m, pltpu.HBM) for m in matrices))


def local(queries, query_tangent, key_rows, key_tangent, value_rows, value_tangent, out_weight):
    k, g_count, head_axis = (lax.axis_size(a) for a in ("k", "g", "head"))
    plane_axes = ("head", "g")
    group = g_count * head_axis
    heads = H // group
    rows = queries.shape[0] * head_axis
    swap = [(0, 1), (1, 0)]

    def within_plane(x):
        return lax.all_to_all(x, plane_axes, split_axis=0, concat_axis=0, tiled=True)

    packed_queries = pack(group, queries, query_tangent)
    plane_queries = within_plane(packed_queries)
    partner = lax.axis_index(("g", "head")).astype(jnp.int32) ^ jnp.arange(group, dtype=jnp.int32)
    order = (partner % head_axis) * g_count + partner // head_axis
    kv = pieces(
        group, order, packed_queries, key_rows, key_tangent, value_rows, value_tangent
    )
    kv = [
        lax.ppermute(piece, ("g", "head"), [(i, i ^ d) for i in range(group)]) if d else piece
        for d, piece in enumerate(kv)
    ]
    if k == 2:
        home_queries = [plane_queries[None], lax.ppermute(plane_queries, "k", swap)[None]]
    else:
        home_queries = [lax.all_gather(plane_queries, "k", axis=0, tiled=False)]
    away_queries = [lax.ppermute(q, "core", swap) for q in home_queries]

    plane = lax.axis_index("k").astype(jnp.int32).reshape(1)
    away, home = (
        attend(some, kv, plane, k, g_count, head_axis).reshape(k * g_count, rows, -1)
        for some in (away_queries, home_queries)
    )
    parts = merge_pair(home, lax.ppermute(away, "core", swap), heads)
    parts = lax.all_to_all(parts, ("k", "g"), split_axis=0, concat_axis=0, tiled=True)
    parts = parts.reshape((k, g_count) + parts.shape[1:])

    width = out_weight.shape[1] // head_axis
    mine = lax.axis_index("head").astype(jnp.int32).reshape(1)
    merged = (2 * rows, out_weight.shape[0])
    merging = functools.partial(first_kernel, heads)
    if head_axis == 2:
        sent, both = project(merging, 1 - mine, parts, out_weight, width, jnp.bfloat16, merged)
        received = lax.ppermute(sent, "head", swap)
        (own,) = project(second_kernel, mine, both, out_weight, width, jnp.float32)
        total = own + received.astype(jnp.float32)
    else:
        partial, _ = project(
            merging, 0 * mine, parts, out_weight, width * head_axis, jnp.float32, merged
        )
        total = lax.psum_scatter(partial, "head", scatter_dimension=1, tiled=True)
    total = total.astype(jnp.bfloat16)
    return (total[:rows], total[rows:])


def solution(mesh):
    blk, head_axis = mesh.shape["blk"], mesh.shape["head"]
    g_count = math.gcd(H // head_axis, blk // 2)
    fine = Mesh(
        mesh.devices.reshape(blk // (2 * g_count), g_count, 2, head_axis),
        ("k", "g", "core", "head"),
    )
    rows = P(("k", "g", "core", "head"), None)
    return jax.shard_map(
        local,
        mesh=fine,
        in_specs=(rows,) * 6 + (P("head", None),),
        out_specs=(P(("k", "g", "core"), "head"),) * 2,
        check_vma=False,
    )
```

```python
import functools
import math

import jax
import jax.numpy as jnp
from jax import lax
from jax.experimental import pallas as pl
from jax.experimental.pallas import tpu as pltpu
from jax.sharding import Mesh, PartitionSpec as P

H = 24
DH = 128
NT = (((1,), (1,)), ((), ()))
TURNS = (0, 6, 1, 5, 2, 7, 4, 3)
ATTEND_VMEM = 24 * 2**20
PROJECT_VMEM = 20 * 2**20


def split_bf16(x, parts):
    terms = []
    for _ in range(parts):
        term = x.astype(jnp.bfloat16)
        terms.append(term)
        x = x - term.astype(jnp.float32)
    return terms


def attend_kernel(heads, row_len, group, plane_ref, *refs):
    query_refs, kv_refs, out_ref = refs[: -group - 1], refs[-group - 1 : -1], refs[-1]
    plane_rows = group * row_len
    g_count, head_axis = out_ref.shape[1], out_ref.shape[2] // row_len
    scale = DH ** (-0.5)

    def some_planes(blocks, planes):
        rows = len(blocks) * plane_rows
        lane = lax.broadcasted_iota(jnp.int32, (rows, DH), 1)
        lse = slopes_mean = jnp.zeros((rows, DH), jnp.float32)

        def put(x, columns):
            for i, plane in enumerate(planes):
                for head in range(head_axis):
                    for g in range(g_count):
                        here = i * plane_rows + (head * g_count + g) * row_len
                        there = slice(head * row_len, (head + 1) * row_len)
                        out_ref[plane, g, there, columns] = x[here : here + row_len]

        for h in range(heads):
            lanes = slice(h * DH, (h + 1) * DH)
            key, key_tan, value, value_tan = (
                jnp.concatenate([ref[t, :, lanes] for ref in kv_refs]) for t in range(4)
            )
            query, qtan = (
                jnp.concatenate(
                    [ref[j, :, t, :, lanes].reshape(plane_rows, DH) for ref, j in blocks]
                )
                for t in range(2)
            )
            scores = lax.dot_general(query, key, NT, preferred_element_type=jnp.float32) * scale
            slopes = (
                lax.dot_general(
                    jnp.concatenate([qtan, query], axis=1),
                    jnp.concatenate([key, key_tan], axis=1),
                    NT,
                    preferred_element_type=jnp.float32,
                )
                * scale
            )
            peak = jnp.max(scores, axis=1, keepdims=True)
            unnormed = jnp.exp(scores - peak)
            tilted = unnormed * slopes
            total = jnp.sum(unnormed, axis=1, keepdims=True)
            slope_sum = jnp.sum(tilted, axis=1, keepdims=True)
            sums = jnp.dot(
                unnormed.astype(jnp.bfloat16),
                jnp.concatenate([value, value_tan], axis=1),
                preferred_element_type=jnp.float32,
            )
            tilted_sum = jnp.dot(
                tilted.astype(jnp.bfloat16), value, preferred_element_type=jnp.float32
            )
            inv = 1.0 / total
            mean_slope = slope_sum * inv
            mean_value = sums[:, :DH] * inv
            tangent = (sums[:, DH:] + tilted_sum) * inv - mean_slope * mean_value
            both = jnp.concatenate([mean_value, tangent], axis=1).astype(jnp.bfloat16)
            put(both, slice(2 * h * DH, 2 * (h + 1) * DH))
            lse = jnp.where(lane == h, peak + jnp.log(total), lse)
            slopes_mean = jnp.where(lane == h, mean_slope, slopes_mean)
        put(packed_stats(lse, slopes_mean, heads), slice(2 * heads * DH, (2 * heads + 1) * DH))

    if len(query_refs) > 1:
        planes = [plane_ref[0] ^ d for d in range(len(query_refs))]
        some_planes([(ref, 0) for ref in query_refs], planes)
    else:
        (ref,) = query_refs
        count = math.gcd(ref.shape[0], 4)

        @pl.loop(0, ref.shape[0] // count)
        def _(step):
            planes = [step * count + j for j in range(count)]
            some_planes([(ref, j) for j in planes], planes)


def attend(queries, kv, plane, k, g_count, head_axis):
    heads = kv[0].shape[2] // DH
    row_len = queries[0].shape[3]
    out_shape = (k, g_count, head_axis * row_len, heads * 2 * DH + DH)
    whole = pl.BlockSpec(memory_space=pltpu.VMEM)
    return pl.pallas_call(
        functools.partial(attend_kernel, heads, row_len, len(kv)),
        out_shape=jax.ShapeDtypeStruct(out_shape, jnp.bfloat16),
        in_specs=[pl.BlockSpec(memory_space=pltpu.SMEM)] + [whole] * (len(queries) + len(kv)),
        out_specs=whole,
        compiler_params=pltpu.CompilerParams(vmem_limit_bytes=ATTEND_VMEM),
        name="attend",
    )(plane, *queries, *kv)


def packed_stats(lse, slope, heads):
    lane = lax.broadcasted_iota(jnp.int32, lse.shape, 1)
    total = 0.0
    terms = split_bf16(jnp.where(lane < heads, lse, 0.0), 3)
    terms += split_bf16(jnp.where(lane < heads, slope, 0.0), 2)
    for i, term in enumerate(terms):
        term = term.astype(jnp.float32)
        total += pltpu.roll(term, i * heads, 1) if i else term
    return total.astype(jnp.bfloat16)


def merge_stats(tails, heads):
    def term(tail, i):
        return pltpu.roll(tail, DH - i * heads, 1) if i else tail

    tails = [tail.astype(jnp.float32) for tail in tails]
    lse = [term(tail, 0) + term(tail, 1) + term(tail, 2) for tail in tails]
    slope = [term(tail, 3) + term(tail, 4) for tail in tails]
    top = functools.reduce(jnp.maximum, lse)
    share = [jnp.exp(e - top) for e in lse]
    total = sum(share)
    inv = 1.0 / total
    share = [e * inv for e in share]
    mean_slope = sum(e * s for e, s in zip(share, slope))
    shift = [e * (s - mean_slope) for e, s in zip(share, slope)]
    return share, shift, top + jnp.log(total), mean_slope


def merge_head(parts, share, shift, h):
    value = tangent = 0.0
    for part, e, s in zip(parts, share, shift):
        own = part[:, 2 * h * DH : (2 * h + 1) * DH].astype(jnp.float32)
        own_tan = part[:, (2 * h + 1) * DH : (2 * h + 2) * DH].astype(jnp.float32)
        e, s = e[:, h : h + 1], s[:, h : h + 1]
        value += e * own
        tangent += e * own_tan + s * own
    return value, tangent


def merge(place_ref, parts_refs, both_ref, heads, g_count):
    rows = parts_refs[0].shape[0]
    tail = slice(2 * heads * DH, (2 * heads + 1) * DH)
    for d in range(g_count):
        g = (place_ref[0] ^ d) % g_count
        parts = [ref[...] for ref in parts_refs[d::g_count]]
        share, shift, _, _ = merge_stats([part[:, tail] for part in parts], heads)
        for h in range(heads):
            value, tangent = merge_head(parts, share, shift, h)
            columns = pl.ds(pl.multiple_of((g * heads + h) * DH, DH), DH)
            both_ref[:rows, columns] = value.astype(jnp.bfloat16)
            both_ref[rows:, columns] = tangent.astype(jnp.bfloat16)


def pair_kernel(heads, place_ref, home_ref, away_ref, *out_refs):
    tail = slice(2 * heads * DH, (2 * heads + 1) * DH)
    for d, out_ref in enumerate(out_refs):
        parts = [ref[place_ref[0] ^ d] for ref in (home_ref, away_ref)]
        share, shift, lse, slope = merge_stats([part[:, tail] for part in parts], heads)
        for h in range(heads):
            both = jnp.concatenate(merge_head(parts, share, shift, h), axis=1)
            out_ref[:, 2 * h * DH : 2 * (h + 1) * DH] = both.astype(jnp.bfloat16)
        out_ref[:, tail] = packed_stats(lse, slope, heads)


def merge_pair(place, home, away, heads):
    whole = pl.BlockSpec(memory_space=pltpu.VMEM)
    count = home.shape[0]
    return pl.pallas_call(
        functools.partial(pair_kernel, heads),
        out_shape=[jax.ShapeDtypeStruct(home.shape[1:], home.dtype)] * count,
        in_specs=[pl.BlockSpec(memory_space=pltpu.SMEM), whole, whole],
        out_specs=[whole] * count,
        compiler_params=pltpu.CompilerParams(vmem_limit_bytes=ATTEND_VMEM),
        name="merge_pair",
    )(place, home, away)


def first_kernel(heads, g_count, half_ref, place_ref, weight_ref, *refs):
    *parts_refs, out_ref, both_ref, held, sems = refs
    copies = fetch(half_ref, weight_ref, held, sems)
    merge(place_ref, parts_refs, both_ref, heads, g_count)
    times_held(copies, both_ref, out_ref, held)


def second_kernel(half_ref, place_ref, weight_ref, both_ref, out_ref, held, sems):
    times_held(fetch(half_ref, weight_ref, held, sems), both_ref, out_ref, held)


def fetch(half_ref, weight_ref, held, sems):
    chunks, _, tile = held.shape
    copies = []
    for i in range(chunks):
        first = pl.multiple_of((half_ref[0] * chunks + i) * tile, tile)
        copy = pltpu.make_async_copy(weight_ref.at[:, pl.ds(first, tile)], held.at[i], sems.at[i])
        copy.start()
        copies.append(copy)
    return copies


def times_held(copies, both_ref, out_ref, held):
    tile = held.shape[2]
    for i, copy in enumerate(copies):
        copy.wait()
        out_ref[:, i * tile : (i + 1) * tile] = jnp.dot(
            both_ref[...], held[i], preferred_element_type=jnp.float32
        ).astype(out_ref.dtype)


def project(kernel, half, place, left, weight, width, dtype, merged=None):
    depth = weight.shape[0]
    chunks = 4
    rows = merged[0] if merged else left[0].shape[0]
    outs = [jax.ShapeDtypeStruct((rows, width), dtype)]
    if merged:
        outs.append(jax.ShapeDtypeStruct(merged, jnp.bfloat16))
    whole = pl.BlockSpec(memory_space=pltpu.VMEM)
    scalar = pl.BlockSpec(memory_space=pltpu.SMEM)
    return pl.pallas_call(
        kernel,
        out_shape=outs,
        in_specs=[scalar, scalar, pl.BlockSpec(memory_space=pl.ANY)] + [whole] * len(left),
        out_specs=[whole] * len(outs),
        scratch_shapes=[
            pltpu.VMEM((chunks, depth, width // chunks), jnp.bfloat16),
            pltpu.SemaphoreType.DMA((chunks,)),
        ],
        compiler_params=pltpu.CompilerParams(vmem_limit_bytes=PROJECT_VMEM),
        cost_estimate=pl.CostEstimate(
            flops=2 * rows * depth * width, bytes_accessed=2 * depth * width, transcendentals=0
        ),
        name="project",
    )(half, place, pltpu.with_memory_space_constraint(weight, pltpu.HBM), *left)


def pack_kernel(turns, g_count, head_axis, place_ref, *refs):
    group = len(turns)
    matrix_refs, query_ref, piece_refs, sems = refs[:6], refs[6], refs[7:-1], refs[-1]
    width = query_ref.shape[3]
    copies = []

    def copy(ref, first, to, *sem):
        columns = pl.ds(pl.multiple_of(first * width, width), width)
        copies.append(pltpu.make_async_copy(ref.at[:, columns], to, sems.at[sem]))

    for i in range(group):
        for t in range(2):
            copy(matrix_refs[t], i, query_ref.at[i, t], i, t)
    for i, turn in enumerate(turns):
        partner = place_ref[0] ^ turn
        column = (partner % head_axis) * g_count + partner // head_axis
        for t in range(4):
            copy(matrix_refs[2 + t], column, piece_refs[i].at[t], i, 2 + t)
    for each in copies:
        each.start()
    for each in copies:
        each.wait()


def pack(turns, g_count, head_axis, place, *matrices):
    group = len(turns)
    rows, columns = matrices[0].shape
    width = columns // group
    piece = jax.ShapeDtypeStruct((4, matrices[2].shape[0], width), jnp.bfloat16)
    outs = [jax.ShapeDtypeStruct((group, 2, rows, width), jnp.bfloat16)] + [piece] * group
    return pl.pallas_call(
        functools.partial(pack_kernel, turns, g_count, head_axis),
        out_shape=outs,
        in_specs=[pl.BlockSpec(memory_space=pltpu.SMEM)]
        + [pl.BlockSpec(memory_space=pl.ANY)] * len(matrices),
        out_specs=[pl.BlockSpec(memory_space=pltpu.VMEM)] * len(outs),
        scratch_shapes=[pltpu.SemaphoreType.DMA((group, len(matrices)))],
        compiler_params=pltpu.CompilerParams(vmem_limit_bytes=8 * 2**20),
        name="pack",
    )(place, *(pltpu.with_memory_space_constraint(m, pltpu.HBM) for m in matrices))


def local(queries, query_tangent, key_rows, key_tangent, value_rows, value_tangent, out_weight):
    k, g_count, head_axis = (lax.axis_size(a) for a in ("k", "g", "head"))
    plane_axes = ("head", "g")
    group = g_count * head_axis
    heads = H // group
    rows = queries.shape[0] * head_axis
    swap = [(0, 1), (1, 0)]

    def within_plane(x):
        return lax.all_to_all(x, plane_axes, split_axis=0, concat_axis=0, tiled=True)

    turns = sorted(range(group), key=TURNS.index)
    in_plane = lax.axis_index(("g", "head")).astype(jnp.int32).reshape(1)
    packed_queries, *kv = pack(
        turns,
        g_count,
        head_axis,
        in_plane,
        queries,
        query_tangent,
        key_rows,
        key_tangent,
        value_rows,
        value_tangent,
    )
    plane_queries = within_plane(packed_queries)
    kv = [
        lax.ppermute(piece, ("g", "head"), [(i, i ^ d) for i in range(group)]) if d else piece
        for d, piece in zip(turns, kv)
    ]
    if k == 2:
        home_queries = [plane_queries[None], lax.ppermute(plane_queries, "k", swap)[None]]
    else:
        home_queries = [lax.all_gather(plane_queries, "k", axis=0, tiled=False)]
    away_queries = [lax.ppermute(q, "core", swap) for q in home_queries]

    plane = lax.axis_index("k").astype(jnp.int32).reshape(1)
    away, home = (
        attend(some, kv, plane, k, g_count, head_axis).reshape(k * g_count, rows, -1)
        for some in (away_queries, home_queries)
    )
    place = lax.axis_index(("k", "g")).astype(jnp.int32).reshape(1)
    parts = merge_pair(place, home, lax.ppermute(away, "core", swap), heads)
    count = k * g_count
    parts = [
        lax.ppermute(part, ("k", "g"), [(i, i ^ d) for i in range(count)]) if d else part
        for d, part in enumerate(parts)
    ]

    width = out_weight.shape[1] // head_axis
    mine = lax.axis_index("head").astype(jnp.int32).reshape(1)
    merged = (2 * rows, out_weight.shape[0])
    merging = functools.partial(first_kernel, heads, g_count)
    if head_axis == 2:
        sent, both = project(
            merging, 1 - mine, place, parts, out_weight, width, jnp.bfloat16, merged
        )
        received = lax.ppermute(sent, "head", swap)
        (own,) = project(second_kernel, mine, place, [both], out_weight, width, jnp.float32)
        total = own + received.astype(jnp.float32)
    else:
        partial, _ = project(
            merging, 0 * mine, place, parts, out_weight, width * head_axis, jnp.float32, merged
        )
        total = lax.psum_scatter(partial, "head", scatter_dimension=1, tiled=True)
    total = total.astype(jnp.bfloat16)
    return (total[:rows], total[rows:])


def solution(mesh):
    blk, head_axis = mesh.shape["blk"], mesh.shape["head"]
    g_count = math.gcd(H // head_axis, blk // 2)
    fine = Mesh(
        mesh.devices.reshape(blk // (2 * g_count), g_count, 2, head_axis),
        ("k", "g", "core", "head"),
    )
    rows = P(("k", "g", "core", "head"), None)
    return jax.shard_map(
        local,
        mesh=fine,
        in_specs=(rows,) * 6 + (P("head", None),),
        out_specs=(P(("k", "g", "core"), "head"),) * 2,
        check_vma=False,
    )
```

```python
import functools
import math

import jax
import jax.numpy as jnp
from jax import lax
from jax.experimental import pallas as pl
from jax.experimental.pallas import tpu as pltpu
from jax.sharding import Mesh, PartitionSpec as P

H = 24
DH = 128
NT = (((1,), (1,)), ((), ()))
PART_TURNS = (4, 6, 5, 7, 1, 2, 3, 0)
HOLD = 4
TURNS = (0, 6, 1, 5, 2, 7, 4, 3)
ATTEND_VMEM = 16 * 2**20
PROJECT_VMEM = 20 * 2**20


def position(device_ref, g_count, head_axis):
    device = device_ref[0]
    pair = 2 * head_axis
    return device // (pair * g_count), device // pair % g_count, device % head_axis


def split_bf16(x, parts):
    terms = []
    for _ in range(parts):
        term = x.astype(jnp.bfloat16)
        terms.append(term)
        x = x - term.astype(jnp.float32)
    return terms


def attend_kernel(heads, row_len, group, device_ref, after_ref, *refs):
    query_refs, kv_refs, out_ref = refs[: -group - 1], refs[-group - 1 : -1], refs[-1]
    plane_rows = group * row_len
    g_count, head_axis = out_ref.shape[1], out_ref.shape[2] // row_len
    scale = DH ** (-0.5)

    def some_planes(blocks, planes):
        rows = len(blocks) * plane_rows
        lane = lax.broadcasted_iota(jnp.int32, (rows, DH), 1)
        lse = slopes_mean = jnp.zeros((rows, DH), jnp.float32)

        def put(x, columns):
            for i, plane in enumerate(planes):
                for head in range(head_axis):
                    for g in range(g_count):
                        here = i * plane_rows + (head * g_count + g) * row_len
                        there = slice(head * row_len, (head + 1) * row_len)
                        out_ref[plane, g, there, columns] = x[here : here + row_len]

        for h in range(heads):
            lanes = slice(h * DH, (h + 1) * DH)
            key, key_tan, value, value_tan = (
                jnp.concatenate([ref[t, :, lanes] for ref in kv_refs]) for t in range(4)
            )
            query, qtan = (
                jnp.concatenate(
                    [ref[j, :, t, :, lanes].reshape(plane_rows, DH) for ref, j in blocks]
                )
                for t in range(2)
            )
            scores = lax.dot_general(query, key, NT, preferred_element_type=jnp.float32) * scale
            slopes = (
                lax.dot_general(
                    jnp.concatenate([qtan, query], axis=1),
                    jnp.concatenate([key, key_tan], axis=1),
                    NT,
                    preferred_element_type=jnp.float32,
                )
                * scale
            )
            peak = jnp.max(scores, axis=1, keepdims=True)
            unnormed = jnp.exp(scores - peak)
            tilted = unnormed * slopes
            total = jnp.sum(unnormed, axis=1, keepdims=True)
            slope_sum = jnp.sum(tilted, axis=1, keepdims=True)
            sums = jnp.dot(
                unnormed.astype(jnp.bfloat16),
                jnp.concatenate([value, value_tan], axis=1),
                preferred_element_type=jnp.float32,
            )
            tilted_sum = jnp.dot(
                tilted.astype(jnp.bfloat16), value, preferred_element_type=jnp.float32
            )
            inv = 1.0 / total
            mean_slope = slope_sum * inv
            mean_value = sums[:, :DH] * inv
            tangent = (sums[:, DH:] + tilted_sum) * inv - mean_slope * mean_value
            both = jnp.concatenate([mean_value, tangent], axis=1).astype(jnp.bfloat16)
            put(both, slice(2 * h * DH, 2 * (h + 1) * DH))
            lse = jnp.where(lane == h, peak + jnp.log(total), lse)
            slopes_mean = jnp.where(lane == h, mean_slope, slopes_mean)
        put(packed_stats(lse, slopes_mean, heads), slice(2 * heads * DH, (2 * heads + 1) * DH))

    if len(query_refs) > 1:
        k, _, _ = position(device_ref, g_count, head_axis)
        planes = [k ^ d for d in range(len(query_refs))]
        some_planes([(ref, 0) for ref in query_refs], planes)
    else:
        (ref,) = query_refs
        count = math.gcd(ref.shape[0], 4)

        @pl.loop(0, ref.shape[0] // count)
        def _(step):
            planes = [step * count + j for j in range(count)]
            some_planes([(ref, j) for j in planes], planes)


def attend(queries, kv, device, k, g_count, head_axis, after):
    heads = kv[0].shape[2] // DH
    row_len = queries[0].shape[3]
    out_shape = (k, g_count, head_axis * row_len, heads * 2 * DH + DH)
    whole = pl.BlockSpec(memory_space=pltpu.VMEM)
    return pl.pallas_call(
        functools.partial(attend_kernel, heads, row_len, len(kv)),
        out_shape=jax.ShapeDtypeStruct(out_shape, jnp.bfloat16),
        in_specs=[pl.BlockSpec(memory_space=pltpu.SMEM), pl.BlockSpec(memory_space=pl.ANY)]
        + [whole] * (len(queries) + len(kv)),
        out_specs=whole,
        compiler_params=pltpu.CompilerParams(vmem_limit_bytes=ATTEND_VMEM),
        name="attend",
    )(device, after, *queries, *kv)


def packed_stats(lse, slope, heads):
    lane = lax.broadcasted_iota(jnp.int32, lse.shape, 1)
    total = 0.0
    terms = split_bf16(jnp.where(lane < heads, lse, 0.0), 3)
    terms += split_bf16(jnp.where(lane < heads, slope, 0.0), 2)
    for i, term in enumerate(terms):
        term = term.astype(jnp.float32)
        total += pltpu.roll(term, i * heads, 1) if i else term
    return total.astype(jnp.bfloat16)


def merge_stats(tails, heads):
    def term(tail, i):
        return pltpu.roll(tail, DH - i * heads, 1) if i else tail

    tails = [tail.astype(jnp.float32) for tail in tails]
    lse = [term(tail, 0) + term(tail, 1) + term(tail, 2) for tail in tails]
    slope = [term(tail, 3) + term(tail, 4) for tail in tails]
    top = functools.reduce(jnp.maximum, lse)
    share = [jnp.exp(e - top) for e in lse]
    total = sum(share)
    inv = 1.0 / total
    share = [e * inv for e in share]
    mean_slope = sum(e * s for e, s in zip(share, slope))
    shift = [e * (s - mean_slope) for e, s in zip(share, slope)]
    return share, shift, top + jnp.log(total), mean_slope


def merge_head(parts, share, shift, h):
    value = tangent = 0.0
    for part, e, s in zip(parts, share, shift):
        own = part[:, 2 * h * DH : (2 * h + 1) * DH].astype(jnp.float32)
        own_tan = part[:, (2 * h + 1) * DH : (2 * h + 2) * DH].astype(jnp.float32)
        e, s = e[:, h : h + 1], s[:, h : h + 1]
        value += e * own
        tangent += e * own_tan + s * own
    return value, tangent


def merge(my_g, parts_refs, both_ref, heads, g_count, turns):
    rows = parts_refs[0].shape[0]
    tail = slice(2 * heads * DH, (2 * heads + 1) * DH)
    for d in range(g_count):
        g = my_g ^ d
        parts = [parts_refs[turns.index(j)][...] for j in range(d, len(turns), g_count)]
        share, shift, _, _ = merge_stats([part[:, tail] for part in parts], heads)
        for h in range(heads):
            value, tangent = merge_head(parts, share, shift, h)
            columns = pl.ds(pl.multiple_of((g * heads + h) * DH, DH), DH)
            both_ref[:rows, columns] = value.astype(jnp.bfloat16)
            both_ref[rows:, columns] = tangent.astype(jnp.bfloat16)


def pair_kernel(heads, turns, g_count, head_axis, device_ref, home_ref, away_ref, *out_refs):
    k, g, _ = position(device_ref, g_count, head_axis)
    tail = slice(2 * heads * DH, (2 * heads + 1) * DH)
    for d, out_ref in zip(turns, out_refs):
        parts = [ref[(k * g_count + g) ^ d] for ref in (home_ref, away_ref)]
        share, shift, lse, slope = merge_stats([part[:, tail] for part in parts], heads)
        for h in range(heads):
            both = jnp.concatenate(merge_head(parts, share, shift, h), axis=1)
            out_ref[:, 2 * h * DH : 2 * (h + 1) * DH] = both.astype(jnp.bfloat16)
        out_ref[:, tail] = packed_stats(lse, slope, heads)


def merge_pair(device, home, away, heads, turns, g_count, head_axis):
    whole = pl.BlockSpec(memory_space=pltpu.VMEM)
    count = home.shape[0]
    return pl.pallas_call(
        functools.partial(pair_kernel, heads, turns, g_count, head_axis),
        out_shape=[jax.ShapeDtypeStruct(home.shape[1:], home.dtype)] * count,
        in_specs=[pl.BlockSpec(memory_space=pltpu.SMEM), whole, whole],
        out_specs=[whole] * count,
        compiler_params=pltpu.CompilerParams(vmem_limit_bytes=ATTEND_VMEM),
        name="merge_pair",
    )(device, home, away)


def first_kernel(heads, g_count, head_axis, turns, held_count, device_ref, weight_ref, *refs):
    _, my_g, _ = position(device_ref, g_count, head_axis)
    if held_count:
        *refs, out_ref, both_ref = refs
        parts_refs, held_refs = refs[:-held_count], refs[-held_count:]
        merge(my_g, parts_refs, both_ref, heads, g_count, turns)
        for i, held in enumerate(held_refs):
            times(both_ref, held[...], out_ref, i)
    else:
        *parts_refs, out_ref, both_ref, held, sems = refs
        copies = fetch(0, weight_ref, held, sems)
        merge(my_g, parts_refs, both_ref, heads, g_count, turns)
        times_held(copies, both_ref, out_ref, held)


def times(both_ref, columns, out_ref, i):
    tile = columns.shape[1]
    out_ref[:, i * tile : (i + 1) * tile] = jnp.dot(
        both_ref[...], columns, preferred_element_type=jnp.float32
    ).astype(out_ref.dtype)


def second_kernel(head_axis, device_ref, weight_ref, both_ref, out_ref, held, sems):
    _, _, head = position(device_ref, 1, head_axis)
    times_held(fetch(head, weight_ref, held, sems), both_ref, out_ref, held)


def fetch(half, weight_ref, held, sems):
    chunks, _, tile = held.shape
    copies = []
    for i in range(chunks):
        first = pl.multiple_of((half * chunks + i) * tile, tile)
        copy = pltpu.make_async_copy(weight_ref.at[:, pl.ds(first, tile)], held.at[i], sems.at[i])
        copy.start()
        copies.append(copy)
    return copies


def times_held(copies, both_ref, out_ref, held):
    for i, copy in enumerate(copies):
        copy.wait()
        times(both_ref, held[i], out_ref, i)


def project(kernel, device, left, weight, width, dtype, merged=None, held=()):
    depth = weight.shape[0]
    chunks = 4
    rows = merged[0] if merged else left[0].shape[0]
    outs = [jax.ShapeDtypeStruct((rows, width), dtype)]
    if merged:
        outs.append(jax.ShapeDtypeStruct(merged, jnp.bfloat16))
    whole = pl.BlockSpec(memory_space=pltpu.VMEM)
    scalar = pl.BlockSpec(memory_space=pltpu.SMEM)
    scratch = [
        pltpu.VMEM((chunks, depth, width // chunks), jnp.bfloat16),
        pltpu.SemaphoreType.DMA((chunks,)),
    ]
    if held:
        scratch = []
    return pl.pallas_call(
        kernel,
        out_shape=outs,
        in_specs=[scalar, pl.BlockSpec(memory_space=pl.ANY)] + [whole] * (len(left) + len(held)),
        out_specs=[whole] * len(outs),
        scratch_shapes=scratch,
        compiler_params=pltpu.CompilerParams(vmem_limit_bytes=PROJECT_VMEM),
        cost_estimate=pl.CostEstimate(
            flops=2 * rows * depth * width, bytes_accessed=2 * depth * width, transcendentals=0
        ),
        name="project",
    )(device, pltpu.with_memory_space_constraint(weight, pltpu.HBM), *left, *held)


def pack_kernel(turns, g_count, head_axis, device_ref, *refs):
    group = len(turns)
    matrix_refs, query_ref, piece_refs, sems = refs[:6], refs[6], refs[7:-1], refs[-1]
    width = query_ref.shape[3]
    _, my_g, head = position(device_ref, g_count, head_axis)
    copies = []

    def copy(ref, first, to, *sem):
        columns = pl.ds(pl.multiple_of(first * width, width), width)
        copies.append(pltpu.make_async_copy(ref.at[:, columns], to, sems.at[sem]))

    for i in range(group):
        for t in range(2):
            copy(matrix_refs[t], i, query_ref.at[i, t], i, t)
    for i, turn in enumerate(turns):
        partner = (my_g * head_axis + head) ^ turn
        column = (partner % head_axis) * g_count + partner // head_axis
        for t in range(4):
            copy(matrix_refs[2 + t], column, piece_refs[i].at[t], i, 2 + t)
    for each in copies:
        each.start()
    for each in copies:
        each.wait()


def pack(turns, g_count, head_axis, device, *matrices):
    group = len(turns)
    rows, columns = matrices[0].shape
    width = columns // group
    piece = jax.ShapeDtypeStruct((4, matrices[2].shape[0], width), jnp.bfloat16)
    outs = [jax.ShapeDtypeStruct((group, 2, rows, width), jnp.bfloat16)] + [piece] * group
    return pl.pallas_call(
        functools.partial(pack_kernel, turns, g_count, head_axis),
        out_shape=outs,
        in_specs=[pl.BlockSpec(memory_space=pltpu.SMEM)]
        + [pl.BlockSpec(memory_space=pl.ANY)] * len(matrices),
        out_specs=[pl.BlockSpec(memory_space=pltpu.VMEM)] * len(outs),
        scratch_shapes=[pltpu.SemaphoreType.DMA((group, len(matrices)))],
        compiler_params=pltpu.CompilerParams(vmem_limit_bytes=8 * 2**20),
        name="pack",
    )(device, *(pltpu.with_memory_space_constraint(m, pltpu.HBM) for m in matrices))


def hold_kernel(head_axis, device_ref, weight_ref, after_ref, out_ref, sems):
    count = sems.shape[0]
    rows, width = out_ref.shape[0] // count, out_ref.shape[1]
    _, _, head = position(device_ref, 1, head_axis)
    columns = pl.ds(pl.multiple_of((1 - head) * width, width), width)
    copies = [
        pltpu.make_async_copy(
            weight_ref.at[pl.ds(i * rows, rows), columns],
            out_ref.at[pl.ds(i * rows, rows)],
            sems.at[i],
        )
        for i in range(count)
    ]
    for copy in copies:
        copy.start()
    for copy in copies:
        copy.wait()


def hold(device, weight, head_axis, after):
    anywhere = pl.BlockSpec(memory_space=pl.ANY)
    width = weight.shape[1] // head_axis
    size = weight.shape[0] * width
    return pl.pallas_call(
        functools.partial(hold_kernel, head_axis),
        out_shape=jax.ShapeDtypeStruct((weight.shape[0], width), weight.dtype),
        in_specs=[pl.BlockSpec(memory_space=pltpu.SMEM), anywhere, anywhere],
        out_specs=pl.BlockSpec(memory_space=pltpu.VMEM),
        scratch_shapes=[pltpu.SemaphoreType.DMA((8,))],
        compiler_params=pltpu.CompilerParams(vmem_limit_bytes=12 * 2**20),
        cost_estimate=pl.CostEstimate(flops=0, bytes_accessed=2 * size, transcendentals=0),
        name="hold",
    )(device, pltpu.with_memory_space_constraint(weight, pltpu.HBM), after)


def local(queries, query_tangent, key_rows, key_tangent, value_rows, value_tangent, out_weight):
    k, g_count, head_axis = (lax.axis_size(a) for a in ("k", "g", "head"))
    plane_axes = ("head", "g")
    group = g_count * head_axis
    heads = H // group
    rows = queries.shape[0] * head_axis
    swap = [(0, 1), (1, 0)]

    def within_plane(x):
        return lax.all_to_all(x, plane_axes, split_axis=0, concat_axis=0, tiled=True)

    turns = sorted(range(group), key=TURNS.index)
    device = lax.axis_index(("k", "g", "core", "head")).astype(jnp.int32).reshape(1)
    packed_queries, *kv = pack(
        turns,
        g_count,
        head_axis,
        device,
        queries,
        query_tangent,
        key_rows,
        key_tangent,
        value_rows,
        value_tangent,
    )
    plane_queries = within_plane(packed_queries)
    kv = [
        lax.ppermute(piece, ("g", "head"), [(i, i ^ d) for i in range(group)]) if d else piece
        for d, piece in zip(turns, kv)
    ]
    if k == 2:
        home_queries = [plane_queries[None], lax.ppermute(plane_queries, "k", swap)[None]]
    else:
        home_queries = [lax.all_gather(plane_queries, "k", axis=0, tiled=False)]
    away_queries = [lax.ppermute(q, "core", swap) for q in home_queries]

    width = out_weight.shape[1] // head_axis
    held = [hold(device, out_weight, head_axis, kv[HOLD])] if head_axis == 2 else []
    away, home = (
        attend(some, kv, device, k, g_count, head_axis, (held + kv)[0])
        for some in (away_queries, home_queries)
    )
    away, home = (some.reshape(k * g_count, rows, -1) for some in (away, home))
    count = k * g_count
    part_turns = PART_TURNS if count == len(PART_TURNS) else tuple(range(count))
    arrived = lax.ppermute(away, "core", swap)
    parts = merge_pair(device, home, arrived, heads, part_turns, g_count, head_axis)
    parts = [
        lax.ppermute(part, ("k", "g"), [(i, i ^ d) for i in range(count)]) if d else part
        for d, part in zip(part_turns, parts)
    ]

    merged = (2 * rows, out_weight.shape[0])
    merging = functools.partial(first_kernel, heads, g_count, head_axis, part_turns, len(held))
    if head_axis == 2:
        sent, both = project(
            merging, device, parts, out_weight, width, jnp.bfloat16, merged, held
        )
        received = lax.ppermute(sent, "head", swap)
        own_half = functools.partial(second_kernel, head_axis)
        (own,) = project(own_half, device, [both], out_weight, width, jnp.float32)
        total = own + received.astype(jnp.float32)
    else:
        partial, _ = project(
            merging, device, parts, out_weight, width * head_axis, jnp.float32, merged
        )
        total = lax.psum_scatter(partial, "head", scatter_dimension=1, tiled=True)
    total = total.astype(jnp.bfloat16)
    return (total[:rows], total[rows:])


def solution(mesh):
    blk, head_axis = mesh.shape["blk"], mesh.shape["head"]
    g_count = math.gcd(H // head_axis, blk // 2)
    fine = Mesh(
        mesh.devices.reshape(blk // (2 * g_count), g_count, 2, head_axis),
        ("k", "g", "core", "head"),
    )
    rows = P(("k", "g", "core", "head"), None)
    return jax.shard_map(
        local,
        mesh=fine,
        in_specs=(rows,) * 6 + (P("head", None),),
        out_specs=(P(("k", "g", "core"), "head"),) * 2,
        check_vma=False,
    )
```

```python
import functools
import math

import jax
import jax.numpy as jnp
from jax import lax
from jax.experimental import pallas as pl
from jax.experimental.pallas import tpu as pltpu
from jax.sharding import Mesh, PartitionSpec as P

H = 24
DH = 128
NT = (((1,), (1,)), ((), ()))
PART_TURNS = (4, 6, 5, 7, 1, 2, 3, 0)
SPLIT = 4
TURNS = (2, 4, 1)
FAR = 7
ATTEND_VMEM = 16 * 2**20
PROJECT_VMEM = 20 * 2**20


def position(device_ref, g_count, head_axis):
    device = device_ref[0]
    pair = 2 * head_axis
    return device // (pair * g_count), device // pair % g_count, device % head_axis


def split_bf16(x, parts):
    terms = []
    for _ in range(parts):
        term = x.astype(jnp.bfloat16)
        terms.append(term)
        x = x - term.astype(jnp.float32)
    return terms


def attend_kernel(heads, row_len, kv_count, device_ref, after_ref, *refs):
    query_refs, kv_refs, out_ref = refs[: -kv_count - 1], refs[-kv_count - 1 : -1], refs[-1]
    g_count, head_axis = out_ref.shape[1], out_ref.shape[2] // row_len
    plane_rows = g_count * head_axis * row_len
    scale = DH ** (-0.5)

    def some_planes(blocks, planes):
        rows = len(blocks) * plane_rows
        lane = lax.broadcasted_iota(jnp.int32, (rows, DH), 1)
        lse = slopes_mean = jnp.zeros((rows, DH), jnp.float32)

        def put(x, columns):
            for i, plane in enumerate(planes):
                for head in range(head_axis):
                    for g in range(g_count):
                        here = i * plane_rows + (head * g_count + g) * row_len
                        there = slice(head * row_len, (head + 1) * row_len)
                        out_ref[plane, g, there, columns] = x[here : here + row_len]

        for h in range(heads):
            lanes = slice(h * DH, (h + 1) * DH)
            key, key_tan, value, value_tan = (
                jnp.concatenate([ref[t, :, lanes] for ref in kv_refs]) for t in range(4)
            )
            query, qtan = (
                jnp.concatenate(
                    [ref[j, :, t, :, lanes].reshape(plane_rows, DH) for ref, j in blocks]
                )
                for t in range(2)
            )
            scores = lax.dot_general(query, key, NT, preferred_element_type=jnp.float32) * scale
            slopes = (
                lax.dot_general(
                    jnp.concatenate([qtan, query], axis=1),
                    jnp.concatenate([key, key_tan], axis=1),
                    NT,
                    preferred_element_type=jnp.float32,
                )
                * scale
            )
            peak = jnp.max(scores, axis=1, keepdims=True)
            unnormed = jnp.exp(scores - peak)
            tilted = unnormed * slopes
            total = jnp.sum(unnormed, axis=1, keepdims=True)
            slope_sum = jnp.sum(tilted, axis=1, keepdims=True)
            sums = jnp.dot(
                unnormed.astype(jnp.bfloat16),
                jnp.concatenate([value, value_tan], axis=1),
                preferred_element_type=jnp.float32,
            )
            tilted_sum = jnp.dot(
                tilted.astype(jnp.bfloat16), value, preferred_element_type=jnp.float32
            )
            inv = 1.0 / total
            mean_slope = slope_sum * inv
            mean_value = sums[:, :DH] * inv
            tangent = (sums[:, DH:] + tilted_sum) * inv - mean_slope * mean_value
            both = jnp.concatenate([mean_value, tangent], axis=1).astype(jnp.bfloat16)
            put(both, slice(2 * h * DH, 2 * (h + 1) * DH))
            lse = jnp.where(lane == h, peak + jnp.log(total), lse)
            slopes_mean = jnp.where(lane == h, mean_slope, slopes_mean)
        put(packed_stats(lse, slopes_mean, heads), slice(2 * heads * DH, (2 * heads + 1) * DH))

    if len(query_refs) > 1:
        k, _, _ = position(device_ref, g_count, head_axis)
        planes = [k ^ d for d in range(len(query_refs))]
        some_planes([(ref, 0) for ref in query_refs], planes)
    else:
        (ref,) = query_refs
        count = math.gcd(ref.shape[0], 4)

        @pl.loop(0, ref.shape[0] // count)
        def _(step):
            planes = [step * count + j for j in range(count)]
            some_planes([(ref, j) for j in planes], planes)


def attend(queries, kv, device, k, g_count, head_axis, after):
    heads = kv[0].shape[2] // DH
    row_len = queries[0].shape[3]
    out_shape = (k, g_count, head_axis * row_len, heads * 2 * DH + DH)
    whole = pl.BlockSpec(memory_space=pltpu.VMEM)
    return pl.pallas_call(
        functools.partial(attend_kernel, heads, row_len, len(kv)),
        out_shape=jax.ShapeDtypeStruct(out_shape, jnp.bfloat16),
        in_specs=[pl.BlockSpec(memory_space=pltpu.SMEM), pl.BlockSpec(memory_space=pl.ANY)]
        + [whole] * (len(queries) + len(kv)),
        out_specs=whole,
        compiler_params=pltpu.CompilerParams(vmem_limit_bytes=ATTEND_VMEM),
        name="attend",
    )(device, after, *queries, *kv)


def packed_stats(lse, slope, heads):
    lane = lax.broadcasted_iota(jnp.int32, lse.shape, 1)
    total = 0.0
    terms = split_bf16(jnp.where(lane < heads, lse, 0.0), 3)
    terms += split_bf16(jnp.where(lane < heads, slope, 0.0), 2)
    for i, term in enumerate(terms):
        term = term.astype(jnp.float32)
        total += pltpu.roll(term, i * heads, 1) if i else term
    return total.astype(jnp.bfloat16)


def merge_stats(tails, heads):
    def term(tail, i):
        return pltpu.roll(tail, DH - i * heads, 1) if i else tail

    tails = [tail.astype(jnp.float32) for tail in tails]
    lse = [term(tail, 0) + term(tail, 1) + term(tail, 2) for tail in tails]
    slope = [term(tail, 3) + term(tail, 4) for tail in tails]
    top = functools.reduce(jnp.maximum, lse)
    share = [jnp.exp(e - top) for e in lse]
    total = sum(share)
    inv = 1.0 / total
    share = [e * inv for e in share]
    mean_slope = sum(e * s for e, s in zip(share, slope))
    shift = [e * (s - mean_slope) for e, s in zip(share, slope)]
    return share, shift, top + jnp.log(total), mean_slope


def merge_head(parts, share, shift, h):
    value = tangent = 0.0
    for part, e, s in zip(parts, share, shift):
        own = part[:, 2 * h * DH : (2 * h + 1) * DH].astype(jnp.float32)
        own_tan = part[:, (2 * h + 1) * DH : (2 * h + 2) * DH].astype(jnp.float32)
        e, s = e[:, h : h + 1], s[:, h : h + 1]
        value += e * own
        tangent += e * own_tan + s * own
    return value, tangent


def merge(my_g, parts_refs, both_ref, heads, g_count, turns):
    rows = parts_refs[0].shape[0]
    tail = slice(2 * heads * DH, (2 * heads + 1) * DH)
    for d in range(g_count):
        g = my_g ^ d
        parts = [parts_refs[turns.index(j)][...] for j in range(d, len(turns), g_count)]
        share, shift, _, _ = merge_stats([part[:, tail] for part in parts], heads)
        for h in range(heads):
            value, tangent = merge_head(parts, share, shift, h)
            columns = pl.ds(pl.multiple_of((g * heads + h) * DH, DH), DH)
            both_ref[:rows, columns] = value.astype(jnp.bfloat16)
            both_ref[rows:, columns] = tangent.astype(jnp.bfloat16)


def pair_kernel(heads, turns, g_count, head_axis, device_ref, home_ref, away_ref, *out_refs):
    k, g, _ = position(device_ref, g_count, head_axis)
    tail = slice(2 * heads * DH, (2 * heads + 1) * DH)
    for d, out_ref in zip(turns, out_refs):
        parts = [ref[(k * g_count + g) ^ d] for ref in (home_ref, away_ref)]
        share, shift, lse, slope = merge_stats([part[:, tail] for part in parts], heads)
        for h in range(heads):
            both = jnp.concatenate(merge_head(parts, share, shift, h), axis=1)
            out_ref[:, 2 * h * DH : 2 * (h + 1) * DH] = both.astype(jnp.bfloat16)
        out_ref[:, tail] = packed_stats(lse, slope, heads)


def merge_pair(device, home, away, heads, turns, g_count, head_axis):
    whole = pl.BlockSpec(memory_space=pltpu.VMEM)
    count = len(turns)
    return pl.pallas_call(
        functools.partial(pair_kernel, heads, turns, g_count, head_axis),
        out_shape=[jax.ShapeDtypeStruct(home.shape[1:], home.dtype)] * count,
        in_specs=[pl.BlockSpec(memory_space=pltpu.SMEM), whole, whole],
        out_specs=[whole] * count,
        compiler_params=pltpu.CompilerParams(vmem_limit_bytes=ATTEND_VMEM),
        name="merge_pair",
    )(device, home, away)


def first_kernel(heads, g_count, head_axis, turns, held_count, device_ref, weight_ref, *refs):
    _, my_g, _ = position(device_ref, g_count, head_axis)
    if held_count:
        *refs, out_ref, both_ref = refs
        parts_refs, held_refs = refs[:-held_count], refs[-held_count:]
        merge(my_g, parts_refs, both_ref, heads, g_count, turns)
        for i, held in enumerate(held_refs):
            times(both_ref, held[...], out_ref, i)
    else:
        *parts_refs, out_ref, both_ref, held, sems = refs
        copies = fetch(0, weight_ref, held, sems)
        merge(my_g, parts_refs, both_ref, heads, g_count, turns)
        times_held(copies, both_ref, out_ref, held)


def times(both_ref, columns, out_ref, i):
    tile = columns.shape[1]
    out_ref[:, i * tile : (i + 1) * tile] = jnp.dot(
        both_ref[...], columns, preferred_element_type=jnp.float32
    ).astype(out_ref.dtype)


def second_kernel(head_axis, device_ref, weight_ref, both_ref, out_ref, held, sems):
    _, _, head = position(device_ref, 1, head_axis)
    times_held(fetch(head, weight_ref, held, sems), both_ref, out_ref, held)


def fetch(half, weight_ref, held, sems):
    chunks, _, tile = held.shape
    copies = []
    for i in range(chunks):
        first = pl.multiple_of((half * chunks + i) * tile, tile)
        copy = pltpu.make_async_copy(weight_ref.at[:, pl.ds(first, tile)], held.at[i], sems.at[i])
        copy.start()
        copies.append(copy)
    return copies


def times_held(copies, both_ref, out_ref, held):
    for i, copy in enumerate(copies):
        copy.wait()
        times(both_ref, held[i], out_ref, i)


def project(kernel, device, left, weight, width, dtype, merged=None, held=()):
    depth = weight.shape[0]
    chunks = 4
    rows = merged[0] if merged else left[0].shape[0]
    outs = [jax.ShapeDtypeStruct((rows, width), dtype)]
    if merged:
        outs.append(jax.ShapeDtypeStruct(merged, jnp.bfloat16))
    whole = pl.BlockSpec(memory_space=pltpu.VMEM)
    scalar = pl.BlockSpec(memory_space=pltpu.SMEM)
    scratch = [
        pltpu.VMEM((chunks, depth, width // chunks), jnp.bfloat16),
        pltpu.SemaphoreType.DMA((chunks,)),
    ]
    if held:
        scratch = []
    return pl.pallas_call(
        kernel,
        out_shape=outs,
        in_specs=[scalar, pl.BlockSpec(memory_space=pl.ANY)] + [whole] * (len(left) + len(held)),
        out_specs=[whole] * len(outs),
        scratch_shapes=scratch,
        compiler_params=pltpu.CompilerParams(vmem_limit_bytes=PROJECT_VMEM),
        cost_estimate=pl.CostEstimate(
            flops=2 * rows * depth * width, bytes_accessed=2 * depth * width, transcendentals=0
        ),
        name="project",
    )(device, pltpu.with_memory_space_constraint(weight, pltpu.HBM), *left, *held)


def pack_kernel(g_count, head_axis, device_ref, *refs):
    matrix_refs, (query_ref, own_ref, far_ref, mine_ref, other_ref) = refs[:6], refs[6:11]
    held_refs, sems = refs[11:-1], refs[-1]
    width = query_ref.shape[3]
    _, g, head = position(device_ref, g_count, head_axis)
    core = device_ref[0] // head_axis % 2
    copies = [
        pltpu.make_async_copy(ref, held, sems.at[i])
        for i, (ref, held) in enumerate(zip(matrix_refs, held_refs))
    ]
    for copy in copies:
        copy.start()
    for t in range(2):
        copies[t].wait()
        for i in range(query_ref.shape[0]):
            query_ref[i, t] = held_refs[t][:, i * width : (i + 1) * width]
    for t in range(4):
        copies[2 + t].wait()

        def piece(turn):
            partner = (g * head_axis + head) ^ turn
            column = (partner % head_axis) * g_count + partner // head_axis
            return held_refs[2 + t][:, pl.ds(pl.multiple_of(column * width, width), width)]

        own_ref[t] = piece(0)
        far_ref[t] = piece(FAR)
        for j, turn in enumerate(TURNS):
            mine_ref[j, t] = piece(turn ^ (FAR * core))
            other_ref[j, t] = piece(turn ^ (FAR * (1 - core)))


def pack(group, g_count, head_axis, device, *matrices):
    rows, columns = matrices[0].shape
    width = columns // group
    piece = (4, matrices[2].shape[0], width)
    shapes = [(group, 2, rows, width), piece, piece] + [(len(TURNS),) + piece] * 2
    return pl.pallas_call(
        functools.partial(pack_kernel, g_count, head_axis),
        out_shape=[jax.ShapeDtypeStruct(shape, jnp.bfloat16) for shape in shapes],
        in_specs=[pl.BlockSpec(memory_space=pltpu.SMEM)]
        + [pl.BlockSpec(memory_space=pl.ANY)] * len(matrices),
        out_specs=[pl.BlockSpec(memory_space=pltpu.VMEM)] * len(shapes),
        scratch_shapes=[pltpu.VMEM(m.shape, m.dtype) for m in matrices]
        + [pltpu.SemaphoreType.DMA((len(matrices),))],
        compiler_params=pltpu.CompilerParams(vmem_limit_bytes=8 * 2**20),
        name="pack",
    )(device, *(pltpu.with_memory_space_constraint(m, pltpu.HBM) for m in matrices))


def join_kernel(mine_ref, theirs_ref, *out_refs):
    rows = mine_ref.shape[2]
    for j, out_ref in enumerate(out_refs):
        out_ref[:, :rows] = mine_ref[j]
        out_ref[:, rows:] = theirs_ref[j]


def join(mine, theirs):
    count, tensors, rows, width = mine.shape
    whole = pl.BlockSpec(memory_space=pltpu.VMEM)
    return pl.pallas_call(
        join_kernel,
        out_shape=[jax.ShapeDtypeStruct((tensors, 2 * rows, width), mine.dtype)] * count,
        in_specs=[whole, whole],
        out_specs=[whole] * count,
        compiler_params=pltpu.CompilerParams(vmem_limit_bytes=8 * 2**20),
        name="join",
    )(mine, theirs)


def across_chips(turn, g_count, head_axis):
    pairs = []
    for n in range(g_count * head_axis):
        for core in range(2):
            m = n ^ turn ^ (FAR * core)
            number = [(i // head_axis * 2 + core) * head_axis + i % head_axis for i in (n, m)]
            pairs.append(tuple(number))
    return pairs


def hold_kernel(head_axis, device_ref, weight_ref, after_ref, out_ref, sems):
    count = sems.shape[0]
    rows, width = out_ref.shape[0] // count, out_ref.shape[1]
    _, _, head = position(device_ref, 1, head_axis)
    columns = pl.ds(pl.multiple_of((1 - head) * width, width), width)
    copies = [
        pltpu.make_async_copy(
            weight_ref.at[pl.ds(i * rows, rows), columns],
            out_ref.at[pl.ds(i * rows, rows)],
            sems.at[i],
        )
        for i in range(count)
    ]
    for copy in copies:
        copy.start()
    for copy in copies:
        copy.wait()


def hold(device, weight, head_axis, after):
    anywhere = pl.BlockSpec(memory_space=pl.ANY)
    width = weight.shape[1] // head_axis
    size = weight.shape[0] * width
    return pl.pallas_call(
        functools.partial(hold_kernel, head_axis),
        out_shape=jax.ShapeDtypeStruct((weight.shape[0], width), weight.dtype),
        in_specs=[pl.BlockSpec(memory_space=pltpu.SMEM), anywhere, anywhere],
        out_specs=pl.BlockSpec(memory_space=pltpu.VMEM),
        scratch_shapes=[pltpu.SemaphoreType.DMA((8,))],
        compiler_params=pltpu.CompilerParams(vmem_limit_bytes=12 * 2**20),
        cost_estimate=pl.CostEstimate(flops=0, bytes_accessed=2 * size, transcendentals=0),
        name="hold",
    )(device, pltpu.with_memory_space_constraint(weight, pltpu.HBM), after)


def local(queries, query_tangent, key_rows, key_tangent, value_rows, value_tangent, out_weight):
    k, g_count, head_axis = (lax.axis_size(a) for a in ("k", "g", "head"))
    plane_axes = ("head", "g")
    group = g_count * head_axis
    heads = H // group
    rows = queries.shape[0] * head_axis
    swap = [(0, 1), (1, 0)]

    def within_plane(x):
        return lax.all_to_all(x, plane_axes, split_axis=0, concat_axis=0, tiled=True)

    device = lax.axis_index(("k", "g", "core", "head")).astype(jnp.int32).reshape(1)
    packed_queries, own, far, mine, other = pack(
        group,
        g_count,
        head_axis,
        device,
        queries,
        query_tangent,
        key_rows,
        key_tangent,
        value_rows,
        value_tangent,
    )
    plane_queries = within_plane(packed_queries)
    pieces = join(mine, lax.ppermute(other, "core", swap))
    kv = [own]
    kv += [
        lax.ppermute(piece, ("g", "core", "head"), across_chips(turn, g_count, head_axis))
        for turn, piece in zip(TURNS, pieces)
    ]
    kv.append(lax.ppermute(far, ("g", "head"), [(i, i ^ FAR) for i in range(group)]))
    if k == 2:
        home_queries = [plane_queries[None], lax.ppermute(plane_queries, "k", swap)[None]]
    else:
        home_queries = [lax.all_gather(plane_queries, "k", axis=0, tiled=False)]
    away_queries = [lax.ppermute(q, "core", swap) for q in home_queries]

    width = out_weight.shape[1] // head_axis
    held = [hold(device, out_weight, head_axis, own)] if head_axis == 2 else []
    away, home = (
        attend(some, kv, device, k, g_count, head_axis, (held + kv)[0])
        for some in (away_queries, home_queries)
    )
    away, home = (some.reshape(k * g_count, rows, -1) for some in (away, home))
    count = k * g_count
    part_turns = PART_TURNS if count == len(PART_TURNS) else tuple(range(count))
    arrived = lax.ppermute(away, "core", swap)
    part_turns = part_turns[SPLIT:] + part_turns[:SPLIT]
    last, first = (
        merge_pair(device, home, arrived, heads, some, g_count, head_axis)
        for some in (part_turns[:-SPLIT], part_turns[-SPLIT:])
    )
    parts = last + first
    parts = [
        lax.ppermute(part, ("k", "g"), [(i, i ^ d) for i in range(count)]) if d else part
        for d, part in zip(part_turns, parts)
    ]

    merged = (2 * rows, out_weight.shape[0])
    merging = functools.partial(first_kernel, heads, g_count, head_axis, part_turns, len(held))
    if head_axis == 2:
        sent, both = project(
            merging, device, parts, out_weight, width, jnp.bfloat16, merged, held
        )
        received = lax.ppermute(sent, "head", swap)
        own_half = functools.partial(second_kernel, head_axis)
        (own,) = project(own_half, device, [both], out_weight, width, jnp.float32)
        total = own + received.astype(jnp.float32)
    else:
        partial, _ = project(
            merging, device, parts, out_weight, width * head_axis, jnp.float32, merged
        )
        total = lax.psum_scatter(partial, "head", scatter_dimension=1, tiled=True)
    total = total.astype(jnp.bfloat16)
    return (total[:rows], total[rows:])


def solution(mesh):
    blk, head_axis = mesh.shape["blk"], mesh.shape["head"]
    g_count = math.gcd(H // head_axis, blk // 2)
    fine = Mesh(
        mesh.devices.reshape(blk // (2 * g_count), g_count, 2, head_axis),
        ("k", "g", "core", "head"),
    )
    rows = P(("k", "g", "core", "head"), None)
    return jax.shard_map(
        local,
        mesh=fine,
        in_specs=(rows,) * 6 + (P("head", None),),
        out_specs=(P(("k", "g", "core"), "head"),) * 2,
        check_vma=False,
    )
```

```python
import functools
import math

import jax
import jax.numpy as jnp
from jax import lax
from jax.experimental import pallas as pl
from jax.experimental.pallas import tpu as pltpu
from jax.sharding import Mesh, PartitionSpec as P

H = 24
DH = 128
NT = (((1,), (1,)), ((), ()))
PART_TURNS = (4, 6, 5, 7, 1, 2, 3, 0)
SPLIT = 4
TURNS = (2, 1, 4)
FAR = 7
ATTEND_VMEM = 16 * 2**20
PROJECT_VMEM = 20 * 2**20


def position(device_ref, g_count, head_axis):
    device = device_ref[0]
    pair = 2 * head_axis
    return device // (pair * g_count), device // pair % g_count, device % head_axis


def split_bf16(x, parts):
    terms = []
    for _ in range(parts):
        term = x.astype(jnp.bfloat16)
        terms.append(term)
        x = x - term.astype(jnp.float32)
    return terms


def attend_kernel(heads, row_len, kv_count, device_ref, after_ref, *refs):
    query_refs, kv_refs, out_ref = refs[: -kv_count - 1], refs[-kv_count - 1 : -1], refs[-1]
    g_count, head_axis = out_ref.shape[1], out_ref.shape[2] // row_len
    plane_rows = g_count * head_axis * row_len
    scale = DH ** (-0.5)

    def some_planes(blocks, planes):
        rows = len(blocks) * plane_rows
        lane = lax.broadcasted_iota(jnp.int32, (rows, DH), 1)
        lse = slopes_mean = jnp.zeros((rows, DH), jnp.float32)

        def put(x, columns):
            for i, plane in enumerate(planes):
                for head in range(head_axis):
                    for g in range(g_count):
                        here = i * plane_rows + (head * g_count + g) * row_len
                        there = slice(head * row_len, (head + 1) * row_len)
                        out_ref[plane, g, there, columns] = x[here : here + row_len]

        for h in range(heads):
            lanes = slice(h * DH, (h + 1) * DH)
            key, key_tan, value, value_tan = (
                jnp.concatenate([ref[t, :, lanes] for ref in kv_refs]) for t in range(4)
            )
            query, qtan = (
                jnp.concatenate(
                    [ref[j, :, t, :, lanes].reshape(plane_rows, DH) for ref, j in blocks]
                )
                for t in range(2)
            )
            scores = lax.dot_general(query, key, NT, preferred_element_type=jnp.float32) * scale
            slopes = (
                lax.dot_general(
                    jnp.concatenate([qtan, query], axis=1),
                    jnp.concatenate([key, key_tan], axis=1),
                    NT,
                    preferred_element_type=jnp.float32,
                )
                * scale
            )
            peak = jnp.max(scores, axis=1, keepdims=True)
            unnormed = jnp.exp(scores - peak)
            tilted = unnormed * slopes
            total = jnp.sum(unnormed, axis=1, keepdims=True)
            slope_sum = jnp.sum(tilted, axis=1, keepdims=True)
            sums = jnp.dot(
                unnormed.astype(jnp.bfloat16),
                jnp.concatenate([value, value_tan], axis=1),
                preferred_element_type=jnp.float32,
            )
            tilted_sum = jnp.dot(
                tilted.astype(jnp.bfloat16), value, preferred_element_type=jnp.float32
            )
            inv = 1.0 / total
            mean_slope = slope_sum * inv
            mean_value = sums[:, :DH] * inv
            tangent = (sums[:, DH:] + tilted_sum) * inv - mean_slope * mean_value
            both = jnp.concatenate([mean_value, tangent], axis=1).astype(jnp.bfloat16)
            put(both, slice(2 * h * DH, 2 * (h + 1) * DH))
            lse = jnp.where(lane == h, peak + jnp.log(total), lse)
            slopes_mean = jnp.where(lane == h, mean_slope, slopes_mean)
        put(packed_stats(lse, slopes_mean, heads), slice(2 * heads * DH, (2 * heads + 1) * DH))

    if len(query_refs) > 1:
        k, _, _ = position(device_ref, g_count, head_axis)
        planes = [k ^ d for d in range(len(query_refs))]
        some_planes([(ref, 0) for ref in query_refs], planes)
    else:
        (ref,) = query_refs
        count = math.gcd(ref.shape[0], 4)

        @pl.loop(0, ref.shape[0] // count)
        def _(step):
            planes = [step * count + j for j in range(count)]
            some_planes([(ref, j) for j in planes], planes)


def attend(queries, kv, device, k, g_count, head_axis, after):
    heads = kv[0].shape[2] // DH
    row_len = queries[0].shape[3]
    out_shape = (k, g_count, head_axis * row_len, heads * 2 * DH + DH)
    whole = pl.BlockSpec(memory_space=pltpu.VMEM)
    return pl.pallas_call(
        functools.partial(attend_kernel, heads, row_len, len(kv)),
        out_shape=jax.ShapeDtypeStruct(out_shape, jnp.bfloat16),
        in_specs=[pl.BlockSpec(memory_space=pltpu.SMEM), pl.BlockSpec(memory_space=pl.ANY)]
        + [whole] * (len(queries) + len(kv)),
        out_specs=whole,
        compiler_params=pltpu.CompilerParams(vmem_limit_bytes=ATTEND_VMEM),
        name="attend",
    )(device, after, *queries, *kv)


def packed_stats(lse, slope, heads):
    lane = lax.broadcasted_iota(jnp.int32, lse.shape, 1)
    total = 0.0
    terms = split_bf16(jnp.where(lane < heads, lse, 0.0), 3)
    terms += split_bf16(jnp.where(lane < heads, slope, 0.0), 2)
    for i, term in enumerate(terms):
        term = term.astype(jnp.float32)
        total += pltpu.roll(term, i * heads, 1) if i else term
    return total.astype(jnp.bfloat16)


def merge_stats(tails, heads):
    def term(tail, i):
        return pltpu.roll(tail, DH - i * heads, 1) if i else tail

    tails = [tail.astype(jnp.float32) for tail in tails]
    lse = [term(tail, 0) + term(tail, 1) + term(tail, 2) for tail in tails]
    slope = [term(tail, 3) + term(tail, 4) for tail in tails]
    top = functools.reduce(jnp.maximum, lse)
    share = [jnp.exp(e - top) for e in lse]
    total = sum(share)
    inv = 1.0 / total
    share = [e * inv for e in share]
    mean_slope = sum(e * s for e, s in zip(share, slope))
    shift = [e * (s - mean_slope) for e, s in zip(share, slope)]
    return share, shift, top + jnp.log(total), mean_slope


def merge_head(parts, share, shift, h):
    value = tangent = 0.0
    for part, e, s in zip(parts, share, shift):
        own = part[:, 2 * h * DH : (2 * h + 1) * DH].astype(jnp.float32)
        own_tan = part[:, (2 * h + 1) * DH : (2 * h + 2) * DH].astype(jnp.float32)
        e, s = e[:, h : h + 1], s[:, h : h + 1]
        value += e * own
        tangent += e * own_tan + s * own
    return value, tangent


def merge(my_g, parts_refs, both_ref, heads, g_count, turns):
    rows = parts_refs[0].shape[0]
    tail = slice(2 * heads * DH, (2 * heads + 1) * DH)
    for d in range(g_count):
        g = my_g ^ d
        parts = [parts_refs[turns.index(j)][...] for j in range(d, len(turns), g_count)]
        share, shift, _, _ = merge_stats([part[:, tail] for part in parts], heads)
        for h in range(heads):
            value, tangent = merge_head(parts, share, shift, h)
            columns = pl.ds(pl.multiple_of((g * heads + h) * DH, DH), DH)
            both_ref[:rows, columns] = value.astype(jnp.bfloat16)
            both_ref[rows:, columns] = tangent.astype(jnp.bfloat16)


def pair_kernel(heads, turns, g_count, head_axis, device_ref, home_ref, away_ref, *out_refs):
    k, g, _ = position(device_ref, g_count, head_axis)
    tail = slice(2 * heads * DH, (2 * heads + 1) * DH)
    for d, out_ref in zip(turns, out_refs):
        parts = [ref[(k * g_count + g) ^ d] for ref in (home_ref, away_ref)]
        share, shift, lse, slope = merge_stats([part[:, tail] for part in parts], heads)
        for h in range(heads):
            both = jnp.concatenate(merge_head(parts, share, shift, h), axis=1)
            out_ref[:, 2 * h * DH : 2 * (h + 1) * DH] = both.astype(jnp.bfloat16)
        out_ref[:, tail] = packed_stats(lse, slope, heads)


def merge_pair(device, home, away, heads, turns, g_count, head_axis):
    whole = pl.BlockSpec(memory_space=pltpu.VMEM)
    count = len(turns)
    return pl.pallas_call(
        functools.partial(pair_kernel, heads, turns, g_count, head_axis),
        out_shape=[jax.ShapeDtypeStruct(home.shape[1:], home.dtype)] * count,
        in_specs=[pl.BlockSpec(memory_space=pltpu.SMEM), whole, whole],
        out_specs=[whole] * count,
        compiler_params=pltpu.CompilerParams(vmem_limit_bytes=ATTEND_VMEM),
        name="merge_pair",
    )(device, home, away)


def first_kernel(heads, g_count, head_axis, turns, held_count, device_ref, weight_ref, *refs):
    _, my_g, _ = position(device_ref, g_count, head_axis)
    if held_count:
        *refs, out_ref, both_ref = refs
        parts_refs, held_refs = refs[:-held_count], refs[-held_count:]
        merge(my_g, parts_refs, both_ref, heads, g_count, turns)
        for i, held in enumerate(held_refs):
            times(both_ref, held[...], out_ref, i)
    else:
        *parts_refs, out_ref, both_ref, held, sems = refs
        copies = fetch(0, weight_ref, held, sems)
        merge(my_g, parts_refs, both_ref, heads, g_count, turns)
        times_held(copies, both_ref, out_ref, held)


def times(both_ref, columns, out_ref, i):
    tile = columns.shape[1]
    out_ref[:, i * tile : (i + 1) * tile] = jnp.dot(
        both_ref[...], columns, preferred_element_type=jnp.float32
    ).astype(out_ref.dtype)


def second_kernel(head_axis, device_ref, weight_ref, both_ref, out_ref, held, sems):
    _, _, head = position(device_ref, 1, head_axis)
    times_held(fetch(head, weight_ref, held, sems), both_ref, out_ref, held)


def fetch(half, weight_ref, held, sems):
    chunks, _, tile = held.shape
    copies = []
    for i in range(chunks):
        first = pl.multiple_of((half * chunks + i) * tile, tile)
        copy = pltpu.make_async_copy(weight_ref.at[:, pl.ds(first, tile)], held.at[i], sems.at[i])
        copy.start()
        copies.append(copy)
    return copies


def times_held(copies, both_ref, out_ref, held):
    for i, copy in enumerate(copies):
        copy.wait()
        times(both_ref, held[i], out_ref, i)


def project(kernel, device, left, weight, width, dtype, merged=None, held=()):
    depth = weight.shape[0]
    chunks = 4
    rows = merged[0] if merged else left[0].shape[0]
    outs = [jax.ShapeDtypeStruct((rows, width), dtype)]
    if merged:
        outs.append(jax.ShapeDtypeStruct(merged, jnp.bfloat16))
    whole = pl.BlockSpec(memory_space=pltpu.VMEM)
    scalar = pl.BlockSpec(memory_space=pltpu.SMEM)
    scratch = [
        pltpu.VMEM((chunks, depth, width // chunks), jnp.bfloat16),
        pltpu.SemaphoreType.DMA((chunks,)),
    ]
    if held:
        scratch = []
    return pl.pallas_call(
        kernel,
        out_shape=outs,
        in_specs=[scalar, pl.BlockSpec(memory_space=pl.ANY)] + [whole] * (len(left) + len(held)),
        out_specs=[whole] * len(outs),
        scratch_shapes=scratch,
        compiler_params=pltpu.CompilerParams(vmem_limit_bytes=PROJECT_VMEM),
        cost_estimate=pl.CostEstimate(
            flops=2 * rows * depth * width, bytes_accessed=2 * depth * width, transcendentals=0
        ),
        name="project",
    )(device, pltpu.with_memory_space_constraint(weight, pltpu.HBM), *left, *held)


def pack_kernel(g_count, head_axis, device_ref, *refs):
    matrix_refs, (query_ref, own_ref, far_ref, mine_ref, other_ref) = refs[:6], refs[6:11]
    held_refs, sems = refs[11:-1], refs[-1]
    width = query_ref.shape[3]
    _, g, head = position(device_ref, g_count, head_axis)
    core = device_ref[0] // head_axis % 2
    copies = [
        pltpu.make_async_copy(ref, held, sems.at[i])
        for i, (ref, held) in enumerate(zip(matrix_refs, held_refs))
    ]
    for copy in copies:
        copy.start()
    for t in range(2):
        copies[t].wait()
        for i in range(query_ref.shape[0]):
            query_ref[i, t] = held_refs[t][:, i * width : (i + 1) * width]
    for t in range(4):
        copies[2 + t].wait()

        def piece(turn):
            partner = (g * head_axis + head) ^ turn
            column = (partner % head_axis) * g_count + partner // head_axis
            return held_refs[2 + t][:, pl.ds(pl.multiple_of(column * width, width), width)]

        own_ref[t] = piece(0)
        far_ref[t] = piece(FAR)
        for j, turn in enumerate(TURNS):
            mine_ref[j, t] = piece(turn ^ (FAR * core))
            other_ref[j, t] = piece(turn ^ (FAR * (1 - core)))


def pack(group, g_count, head_axis, device, *matrices):
    rows, columns = matrices[0].shape
    width = columns // group
    piece = (4, matrices[2].shape[0], width)
    shapes = [(group, 2, rows, width), piece, piece] + [(len(TURNS),) + piece] * 2
    return pl.pallas_call(
        functools.partial(pack_kernel, g_count, head_axis),
        out_shape=[jax.ShapeDtypeStruct(shape, jnp.bfloat16) for shape in shapes],
        in_specs=[pl.BlockSpec(memory_space=pltpu.SMEM)]
        + [pl.BlockSpec(memory_space=pl.ANY)] * len(matrices),
        out_specs=[pl.BlockSpec(memory_space=pltpu.VMEM)] * len(shapes),
        scratch_shapes=[pltpu.VMEM(m.shape, m.dtype) for m in matrices]
        + [pltpu.SemaphoreType.DMA((len(matrices),))],
        compiler_params=pltpu.CompilerParams(vmem_limit_bytes=8 * 2**20),
        name="pack",
    )(device, *(pltpu.with_memory_space_constraint(m, pltpu.HBM) for m in matrices))


def join_kernel(mine_ref, theirs_ref, *out_refs):
    rows = mine_ref.shape[2]
    for j, out_ref in enumerate(out_refs):
        out_ref[:, :rows] = mine_ref[j]
        out_ref[:, rows:] = theirs_ref[j]


def join(mine, theirs):
    count, tensors, rows, width = mine.shape
    whole = pl.BlockSpec(memory_space=pltpu.VMEM)
    return pl.pallas_call(
        join_kernel,
        out_shape=[jax.ShapeDtypeStruct((tensors, 2 * rows, width), mine.dtype)] * count,
        in_specs=[whole, whole],
        out_specs=[whole] * count,
        compiler_params=pltpu.CompilerParams(vmem_limit_bytes=8 * 2**20),
        name="join",
    )(mine, theirs)


def across_chips(turn, g_count, head_axis):
    pairs = []
    for n in range(g_count * head_axis):
        for core in range(2):
            m = n ^ turn ^ (FAR * core)
            number = [(i // head_axis * 2 + core) * head_axis + i % head_axis for i in (n, m)]
            pairs.append(tuple(number))
    return pairs


def hold_kernel(head_axis, device_ref, weight_ref, after_ref, out_ref, sems):
    count = sems.shape[0]
    rows, width = out_ref.shape[0] // count, out_ref.shape[1]
    _, _, head = position(device_ref, 1, head_axis)
    columns = pl.ds(pl.multiple_of((1 - head) * width, width), width)
    copies = [
        pltpu.make_async_copy(
            weight_ref.at[pl.ds(i * rows, rows), columns],
            out_ref.at[pl.ds(i * rows, rows)],
            sems.at[i],
        )
        for i in range(count)
    ]
    for copy in copies:
        copy.start()
    for copy in copies:
        copy.wait()


def hold(device, weight, head_axis, after):
    anywhere = pl.BlockSpec(memory_space=pl.ANY)
    width = weight.shape[1] // head_axis
    size = weight.shape[0] * width
    return pl.pallas_call(
        functools.partial(hold_kernel, head_axis),
        out_shape=jax.ShapeDtypeStruct((weight.shape[0], width), weight.dtype),
        in_specs=[pl.BlockSpec(memory_space=pltpu.SMEM), anywhere, anywhere],
        out_specs=pl.BlockSpec(memory_space=pltpu.VMEM),
        scratch_shapes=[pltpu.SemaphoreType.DMA((8,))],
        compiler_params=pltpu.CompilerParams(vmem_limit_bytes=12 * 2**20),
        cost_estimate=pl.CostEstimate(flops=0, bytes_accessed=2 * size, transcendentals=0),
        name="hold",
    )(device, pltpu.with_memory_space_constraint(weight, pltpu.HBM), after)


def local(queries, query_tangent, key_rows, key_tangent, value_rows, value_tangent, out_weight):
    k, g_count, head_axis = (lax.axis_size(a) for a in ("k", "g", "head"))
    plane_axes = ("head", "g")
    group = g_count * head_axis
    heads = H // group
    rows = queries.shape[0] * head_axis
    swap = [(0, 1), (1, 0)]

    def within_plane(x):
        return lax.all_to_all(x, plane_axes, split_axis=0, concat_axis=0, tiled=True)

    device = lax.axis_index(("k", "g", "core", "head")).astype(jnp.int32).reshape(1)
    packed_queries, own, far, mine, other = pack(
        group,
        g_count,
        head_axis,
        device,
        queries,
        query_tangent,
        key_rows,
        key_tangent,
        value_rows,
        value_tangent,
    )
    plane_queries = within_plane(packed_queries)
    pieces = join(mine, lax.ppermute(other, "core", swap))
    kv = [own]
    kv += [
        lax.ppermute(piece, ("g", "core", "head"), across_chips(turn, g_count, head_axis))
        for turn, piece in zip(TURNS, pieces)
    ]
    kv.append(lax.ppermute(far, ("g", "head"), [(i, i ^ FAR) for i in range(group)]))
    if k == 2:
        home_queries = [plane_queries[None], lax.ppermute(plane_queries, "k", swap)[None]]
    else:
        home_queries = [lax.all_gather(plane_queries, "k", axis=0, tiled=False)]
    away_queries = [lax.ppermute(q, "core", swap) for q in home_queries]

    width = out_weight.shape[1] // head_axis
    held = [hold(device, out_weight, head_axis, own)] if head_axis == 2 else []
    away, home = (
        attend(some, kv, device, k, g_count, head_axis, (held + kv)[0])
        for some in (away_queries, home_queries)
    )
    away, home = (some.reshape(k * g_count, rows, -1) for some in (away, home))
    count = k * g_count
    part_turns = PART_TURNS if count == len(PART_TURNS) else tuple(range(count))
    arrived = lax.ppermute(away, "core", swap)
    part_turns = part_turns[SPLIT:] + part_turns[:SPLIT]
    last, first = (
        merge_pair(device, home, arrived, heads, some, g_count, head_axis)
        for some in (part_turns[:-SPLIT], part_turns[-SPLIT:])
    )
    parts = last + first
    parts = [
        lax.ppermute(part, ("k", "g"), [(i, i ^ d) for i in range(count)]) if d else part
        for d, part in zip(part_turns, parts)
    ]

    merged = (2 * rows, out_weight.shape[0])
    merging = functools.partial(first_kernel, heads, g_count, head_axis, part_turns, len(held))
    if head_axis == 2:
        sent, both = project(
            merging, device, parts, out_weight, width, jnp.bfloat16, merged, held
        )
        received = lax.ppermute(sent, "head", swap)
        own_half = functools.partial(second_kernel, head_axis)
        (own,) = project(own_half, device, [both], out_weight, width, jnp.float32)
        total = own + received.astype(jnp.float32)
    else:
        partial, _ = project(
            merging, device, parts, out_weight, width * head_axis, jnp.float32, merged
        )
        total = lax.psum_scatter(partial, "head", scatter_dimension=1, tiled=True)
    total = total.astype(jnp.bfloat16)
    return (total[:rows], total[rows:])


def solution(mesh):
    blk, head_axis = mesh.shape["blk"], mesh.shape["head"]
    g_count = math.gcd(H // head_axis, blk // 2)
    fine = Mesh(
        mesh.devices.reshape(blk // (2 * g_count), g_count, 2, head_axis),
        ("k", "g", "core", "head"),
    )
    rows = P(("k", "g", "core", "head"), None)
    return jax.shard_map(
        local,
        mesh=fine,
        in_specs=(rows,) * 6 + (P("head", None),),
        out_specs=(P(("k", "g", "core"), "head"),) * 2,
        check_vma=False,
    )
```

```python
import functools
import math

import jax
import jax.numpy as jnp
from jax import lax
from jax.experimental import pallas as pl
from jax.experimental.pallas import tpu as pltpu
from jax.sharding import Mesh, PartitionSpec as P

H = 24
DH = 128
NT = (((1,), (1,)), ((), ()))
PART_TURNS = (4, 6, 5, 7, 1, 2, 3, 0)
SPLIT = 4
TURNS = (2, 1, 4)
FAR = 7
ATTEND_VMEM = 16 * 2**20
PROJECT_VMEM = 20 * 2**20


def position(device_ref, g_count, head_axis):
    device = device_ref[0]
    pair = 2 * head_axis
    return device // (pair * g_count), device // pair % g_count, device % head_axis


def split_bf16(x, parts):
    terms = []
    for _ in range(parts):
        term = x.astype(jnp.bfloat16)
        terms.append(term)
        x = x - term.astype(jnp.float32)
    return terms


def attend_kernel(heads, row_len, kv_count, device_ref, after_ref, *refs):
    query_refs, kv_refs, out_ref = refs[: -kv_count - 1], refs[-kv_count - 1 : -1], refs[-1]
    g_count, head_axis = out_ref.shape[1], out_ref.shape[2] // row_len
    plane_rows = g_count * head_axis * row_len
    scale = DH ** (-0.5)

    def some_planes(blocks, planes):
        rows = len(blocks) * plane_rows
        lane = lax.broadcasted_iota(jnp.int32, (rows, DH), 1)
        lse = slopes_mean = jnp.zeros((rows, DH), jnp.float32)

        def put(x, columns):
            for i, plane in enumerate(planes):
                for head in range(head_axis):
                    for g in range(g_count):
                        here = i * plane_rows + (head * g_count + g) * row_len
                        there = slice(head * row_len, (head + 1) * row_len)
                        out_ref[plane, g, there, columns] = x[here : here + row_len]

        for h in range(heads):
            lanes = slice(h * DH, (h + 1) * DH)
            key, key_tan, value, value_tan = (
                jnp.concatenate([ref[t, :, lanes] for ref in kv_refs]) for t in range(4)
            )
            query, qtan = (
                jnp.concatenate(
                    [ref[j, :, t, :, lanes].reshape(plane_rows, DH) for ref, j in blocks]
                )
                for t in range(2)
            )
            scores = lax.dot_general(query, key, NT, preferred_element_type=jnp.float32) * scale
            slopes = (
                lax.dot_general(
                    jnp.concatenate([qtan, query], axis=1),
                    jnp.concatenate([key, key_tan], axis=1),
                    NT,
                    preferred_element_type=jnp.float32,
                )
                * scale
            )
            peak = jnp.max(scores, axis=1, keepdims=True)
            unnormed = jnp.exp(scores - peak)
            tilted = unnormed * slopes
            total = jnp.sum(unnormed, axis=1, keepdims=True)
            slope_sum = jnp.sum(tilted, axis=1, keepdims=True)
            sums = jnp.dot(
                unnormed.astype(jnp.bfloat16),
                jnp.concatenate([value, value_tan], axis=1),
                preferred_element_type=jnp.float32,
            )
            tilted_sum = jnp.dot(
                tilted.astype(jnp.bfloat16), value, preferred_element_type=jnp.float32
            )
            inv = 1.0 / total
            mean_slope = slope_sum * inv
            mean_value = sums[:, :DH] * inv
            tangent = (sums[:, DH:] + tilted_sum) * inv - mean_slope * mean_value
            both = jnp.concatenate([mean_value, tangent], axis=1).astype(jnp.bfloat16)
            put(both, slice(2 * h * DH, 2 * (h + 1) * DH))
            lse = jnp.where(lane == h, peak + jnp.log(total), lse)
            slopes_mean = jnp.where(lane == h, mean_slope, slopes_mean)
        put(packed_stats(lse, slopes_mean, heads), slice(2 * heads * DH, (2 * heads + 1) * DH))

    if len(query_refs) > 1:
        k, _, _ = position(device_ref, g_count, head_axis)
        planes = [k ^ d for d in range(len(query_refs))]
        some_planes([(ref, 0) for ref in query_refs], planes)
    else:
        (ref,) = query_refs
        count = math.gcd(ref.shape[0], 4)

        @pl.loop(0, ref.shape[0] // count)
        def _(step):
            planes = [step * count + j for j in range(count)]
            some_planes([(ref, j) for j in planes], planes)


def attend(queries, kv, device, k, g_count, head_axis, after):
    heads = kv[0].shape[2] // DH
    row_len = queries[0].shape[3]
    out_shape = (k, g_count, head_axis * row_len, heads * 2 * DH + DH)
    whole = pl.BlockSpec(memory_space=pltpu.VMEM)
    return pl.pallas_call(
        functools.partial(attend_kernel, heads, row_len, len(kv)),
        out_shape=jax.ShapeDtypeStruct(out_shape, jnp.bfloat16),
        in_specs=[pl.BlockSpec(memory_space=pltpu.SMEM), pl.BlockSpec(memory_space=pl.ANY)]
        + [whole] * (len(queries) + len(kv)),
        out_specs=whole,
        compiler_params=pltpu.CompilerParams(vmem_limit_bytes=ATTEND_VMEM),
        name="attend",
    )(device, after, *queries, *kv)


def packed_stats(lse, slope, heads):
    lane = lax.broadcasted_iota(jnp.int32, lse.shape, 1)
    total = 0.0
    terms = split_bf16(jnp.where(lane < heads, lse, 0.0), 3)
    terms += split_bf16(jnp.where(lane < heads, slope, 0.0), 2)
    for i, term in enumerate(terms):
        term = term.astype(jnp.float32)
        total += pltpu.roll(term, i * heads, 1) if i else term
    return total.astype(jnp.bfloat16)


def merge_stats(tails, heads):
    def term(tail, i):
        return pltpu.roll(tail, DH - i * heads, 1) if i else tail

    tails = [tail.astype(jnp.float32) for tail in tails]
    lse = [term(tail, 0) + term(tail, 1) + term(tail, 2) for tail in tails]
    slope = [term(tail, 3) + term(tail, 4) for tail in tails]
    top = functools.reduce(jnp.maximum, lse)
    share = [jnp.exp(e - top) for e in lse]
    total = sum(share)
    inv = 1.0 / total
    share = [e * inv for e in share]
    mean_slope = sum(e * s for e, s in zip(share, slope))
    shift = [e * (s - mean_slope) for e, s in zip(share, slope)]
    return share, shift, top + jnp.log(total), mean_slope


def merge_head(parts, share, shift, h):
    value = tangent = 0.0
    for part, e, s in zip(parts, share, shift):
        own = part[:, 2 * h * DH : (2 * h + 1) * DH].astype(jnp.float32)
        own_tan = part[:, (2 * h + 1) * DH : (2 * h + 2) * DH].astype(jnp.float32)
        e, s = e[:, h : h + 1], s[:, h : h + 1]
        value += e * own
        tangent += e * own_tan + s * own
    return value, tangent


def merge(my_g, parts_refs, both_ref, heads, g_count, turns):
    rows = parts_refs[0].shape[0]
    tail = slice(2 * heads * DH, (2 * heads + 1) * DH)
    for d in range(g_count):
        g = my_g ^ d
        parts = [parts_refs[turns.index(j)][...] for j in range(d, len(turns), g_count)]
        share, shift, _, _ = merge_stats([part[:, tail] for part in parts], heads)
        for h in range(heads):
            value, tangent = merge_head(parts, share, shift, h)
            columns = pl.ds(pl.multiple_of((g * heads + h) * DH, DH), DH)
            both_ref[:rows, columns] = value.astype(jnp.bfloat16)
            both_ref[rows:, columns] = tangent.astype(jnp.bfloat16)


def pair_kernel(heads, turns, g_count, head_axis, device_ref, home_ref, away_ref, *out_refs):
    k, g, _ = position(device_ref, g_count, head_axis)
    tail = slice(2 * heads * DH, (2 * heads + 1) * DH)
    for d, out_ref in zip(turns, out_refs):
        parts = [ref[(k * g_count + g) ^ d] for ref in (home_ref, away_ref)]
        share, shift, lse, slope = merge_stats([part[:, tail] for part in parts], heads)
        for h in range(heads):
            both = jnp.concatenate(merge_head(parts, share, shift, h), axis=1)
            out_ref[:, 2 * h * DH : 2 * (h + 1) * DH] = both.astype(jnp.bfloat16)
        out_ref[:, tail] = packed_stats(lse, slope, heads)


def merge_pair(device, home, away, heads, turns, g_count, head_axis):
    whole = pl.BlockSpec(memory_space=pltpu.VMEM)
    count = len(turns)
    return pl.pallas_call(
        functools.partial(pair_kernel, heads, turns, g_count, head_axis),
        out_shape=[jax.ShapeDtypeStruct(home.shape[1:], home.dtype)] * count,
        in_specs=[pl.BlockSpec(memory_space=pltpu.SMEM), whole, whole],
        out_specs=[whole] * count,
        compiler_params=pltpu.CompilerParams(vmem_limit_bytes=ATTEND_VMEM),
        name="merge_pair",
    )(device, home, away)


def first_kernel(heads, g_count, head_axis, turns, held_count, device_ref, weight_ref, *refs):
    _, my_g, _ = position(device_ref, g_count, head_axis)
    if held_count:
        *refs, out_ref, both_ref = refs
        parts_refs, held_refs = refs[:-held_count], refs[-held_count:]
        merge(my_g, parts_refs, both_ref, heads, g_count, turns)
        for held in held_refs:
            times(both_ref, held[:, : out_ref.shape[1]], out_ref, 0)
    else:
        *parts_refs, out_ref, both_ref, held, sems = refs
        copies = fetch(0, weight_ref, held, sems)
        merge(my_g, parts_refs, both_ref, heads, g_count, turns)
        times_held(copies, both_ref, out_ref, held)


def times(both_ref, columns, out_ref, i):
    tile = columns.shape[1]
    out_ref[:, i * tile : (i + 1) * tile] = jnp.dot(
        both_ref[...], columns, preferred_element_type=jnp.float32
    ).astype(out_ref.dtype)


def rest_kernel(device_ref, weight_ref, both_ref, held_ref, out_ref):
    times(both_ref, held_ref[:, held_ref.shape[1] - out_ref.shape[1] :], out_ref, 0)


def sum_kernel(own_ref, received_ref, *refs):
    rows = own_ref.shape[0] // 2
    total = (own_ref[...] + received_ref[...].astype(jnp.float32)).astype(jnp.bfloat16)
    refs[-2][...] = total[:rows]
    refs[-1][...] = total[rows:]


def sum_columns(own, received, part, outs=()):
    rows, tile = own.shape[0] // 2, received.shape[1]
    shape = jax.ShapeDtypeStruct((rows, own.shape[1]), jnp.bfloat16)
    return pl.pallas_call(
        sum_kernel,
        grid=(1,),
        out_shape=[shape] * 2,
        in_specs=[
            pl.BlockSpec((2 * rows, tile), lambda n: (0, part)),
            pl.BlockSpec((2 * rows, tile), lambda n: (0, 0)),
        ]
        + [pl.BlockSpec(memory_space=pl.ANY)] * len(outs),
        out_specs=[pl.BlockSpec((rows, tile), lambda n: (0, part))] * 2,
        input_output_aliases={2 + i: i for i in range(len(outs))},
        compiler_params=pltpu.CompilerParams(vmem_limit_bytes=8 * 2**20),
        name="sum_columns",
    )(own, received, *outs)


def second_kernel(head_axis, device_ref, weight_ref, both_ref, out_ref, held, sems):
    _, _, head = position(device_ref, 1, head_axis)
    times_held(fetch(head, weight_ref, held, sems), both_ref, out_ref, held)


def fetch(half, weight_ref, held, sems):
    chunks, _, tile = held.shape
    copies = []
    for i in range(chunks):
        first = pl.multiple_of((half * chunks + i) * tile, tile)
        copy = pltpu.make_async_copy(weight_ref.at[:, pl.ds(first, tile)], held.at[i], sems.at[i])
        copy.start()
        copies.append(copy)
    return copies


def times_held(copies, both_ref, out_ref, held):
    for i, copy in enumerate(copies):
        copy.wait()
        times(both_ref, held[i], out_ref, i)


def project(kernel, device, left, weight, width, dtype, merged=None, held=()):
    depth = weight.shape[0]
    chunks = 4
    rows = merged[0] if merged else left[0].shape[0]
    outs = [jax.ShapeDtypeStruct((rows, width), dtype)]
    if merged:
        outs.append(jax.ShapeDtypeStruct(merged, jnp.bfloat16))
    whole = pl.BlockSpec(memory_space=pltpu.VMEM)
    scalar = pl.BlockSpec(memory_space=pltpu.SMEM)
    scratch = [
        pltpu.VMEM((chunks, depth, width // chunks), jnp.bfloat16),
        pltpu.SemaphoreType.DMA((chunks,)),
    ]
    if held:
        scratch = []
    return pl.pallas_call(
        kernel,
        out_shape=outs,
        in_specs=[scalar, pl.BlockSpec(memory_space=pl.ANY)] + [whole] * (len(left) + len(held)),
        out_specs=[whole] * len(outs),
        scratch_shapes=scratch,
        compiler_params=pltpu.CompilerParams(vmem_limit_bytes=PROJECT_VMEM),
        cost_estimate=pl.CostEstimate(
            flops=2 * rows * depth * width, bytes_accessed=2 * depth * width, transcendentals=0
        ),
        name="project",
    )(device, pltpu.with_memory_space_constraint(weight, pltpu.HBM), *left, *held)


def pack_kernel(g_count, head_axis, device_ref, *refs):
    matrix_refs, (query_ref, own_ref, far_ref, mine_ref, other_ref) = refs[:6], refs[6:11]
    held_refs, sems = refs[11:-1], refs[-1]
    width = query_ref.shape[3]
    _, g, head = position(device_ref, g_count, head_axis)
    core = device_ref[0] // head_axis % 2
    copies = [
        pltpu.make_async_copy(ref, held, sems.at[i])
        for i, (ref, held) in enumerate(zip(matrix_refs, held_refs))
    ]
    for copy in copies:
        copy.start()
    for t in range(2):
        copies[t].wait()
        for i in range(query_ref.shape[0]):
            query_ref[i, t] = held_refs[t][:, i * width : (i + 1) * width]
    for t in range(4):
        copies[2 + t].wait()

        def piece(turn):
            partner = (g * head_axis + head) ^ turn
            column = (partner % head_axis) * g_count + partner // head_axis
            return held_refs[2 + t][:, pl.ds(pl.multiple_of(column * width, width), width)]

        own_ref[t] = piece(0)
        far_ref[t] = piece(FAR)
        for j, turn in enumerate(TURNS):
            mine_ref[j, t] = piece(turn ^ (FAR * core))
            other_ref[j, t] = piece(turn ^ (FAR * (1 - core)))


def pack(group, g_count, head_axis, device, *matrices):
    rows, columns = matrices[0].shape
    width = columns // group
    piece = (4, matrices[2].shape[0], width)
    shapes = [(group, 2, rows, width), piece, piece] + [(len(TURNS),) + piece] * 2
    return pl.pallas_call(
        functools.partial(pack_kernel, g_count, head_axis),
        out_shape=[jax.ShapeDtypeStruct(shape, jnp.bfloat16) for shape in shapes],
        in_specs=[pl.BlockSpec(memory_space=pltpu.SMEM)]
        + [pl.BlockSpec(memory_space=pl.ANY)] * len(matrices),
        out_specs=[pl.BlockSpec(memory_space=pltpu.VMEM)] * len(shapes),
        scratch_shapes=[pltpu.VMEM(m.shape, m.dtype) for m in matrices]
        + [pltpu.SemaphoreType.DMA((len(matrices),))],
        compiler_params=pltpu.CompilerParams(vmem_limit_bytes=8 * 2**20),
        name="pack",
    )(device, *(pltpu.with_memory_space_constraint(m, pltpu.HBM) for m in matrices))


def join_kernel(mine_ref, theirs_ref, *out_refs):
    rows = mine_ref.shape[2]
    for j, out_ref in enumerate(out_refs):
        out_ref[:, :rows] = mine_ref[j]
        out_ref[:, rows:] = theirs_ref[j]


def join(mine, theirs):
    count, tensors, rows, width = mine.shape
    whole = pl.BlockSpec(memory_space=pltpu.VMEM)
    return pl.pallas_call(
        join_kernel,
        out_shape=[jax.ShapeDtypeStruct((tensors, 2 * rows, width), mine.dtype)] * count,
        in_specs=[whole, whole],
        out_specs=[whole] * count,
        compiler_params=pltpu.CompilerParams(vmem_limit_bytes=8 * 2**20),
        name="join",
    )(mine, theirs)


def across_chips(turn, g_count, head_axis):
    pairs = []
    for n in range(g_count * head_axis):
        for core in range(2):
            m = n ^ turn ^ (FAR * core)
            number = [(i // head_axis * 2 + core) * head_axis + i % head_axis for i in (n, m)]
            pairs.append(tuple(number))
    return pairs


def hold_kernel(head_axis, device_ref, weight_ref, after_ref, out_ref, sems):
    count = sems.shape[0]
    rows, width = out_ref.shape[0] // count, out_ref.shape[1]
    _, _, head = position(device_ref, 1, head_axis)
    columns = pl.ds(pl.multiple_of((1 - head) * width, width), width)
    copies = [
        pltpu.make_async_copy(
            weight_ref.at[pl.ds(i * rows, rows), columns],
            out_ref.at[pl.ds(i * rows, rows)],
            sems.at[i],
        )
        for i in range(count)
    ]
    for copy in copies:
        copy.start()
    for copy in copies:
        copy.wait()


def hold(device, weight, head_axis, after):
    anywhere = pl.BlockSpec(memory_space=pl.ANY)
    width = weight.shape[1] // head_axis
    size = weight.shape[0] * width
    return pl.pallas_call(
        functools.partial(hold_kernel, head_axis),
        out_shape=jax.ShapeDtypeStruct((weight.shape[0], width), weight.dtype),
        in_specs=[pl.BlockSpec(memory_space=pltpu.SMEM), anywhere, anywhere],
        out_specs=pl.BlockSpec(memory_space=pltpu.VMEM),
        scratch_shapes=[pltpu.SemaphoreType.DMA((8,))],
        compiler_params=pltpu.CompilerParams(vmem_limit_bytes=12 * 2**20),
        cost_estimate=pl.CostEstimate(flops=0, bytes_accessed=2 * size, transcendentals=0),
        name="hold",
    )(device, pltpu.with_memory_space_constraint(weight, pltpu.HBM), after)


def local(queries, query_tangent, key_rows, key_tangent, value_rows, value_tangent, out_weight):
    k, g_count, head_axis = (lax.axis_size(a) for a in ("k", "g", "head"))
    plane_axes = ("head", "g")
    group = g_count * head_axis
    heads = H // group
    rows = queries.shape[0] * head_axis
    swap = [(0, 1), (1, 0)]

    def within_plane(x):
        return lax.all_to_all(x, plane_axes, split_axis=0, concat_axis=0, tiled=True)

    device = lax.axis_index(("k", "g", "core", "head")).astype(jnp.int32).reshape(1)
    packed_queries, own, far, mine, other = pack(
        group,
        g_count,
        head_axis,
        device,
        queries,
        query_tangent,
        key_rows,
        key_tangent,
        value_rows,
        value_tangent,
    )
    plane_queries = within_plane(packed_queries)
    pieces = join(mine, lax.ppermute(other, "core", swap))
    kv = [own]
    kv += [
        lax.ppermute(piece, ("g", "core", "head"), across_chips(turn, g_count, head_axis))
        for turn, piece in zip(TURNS, pieces)
    ]
    kv.append(lax.ppermute(far, ("g", "head"), [(i, i ^ FAR) for i in range(group)]))
    if k == 2:
        home_queries = [plane_queries[None], lax.ppermute(plane_queries, "k", swap)[None]]
    else:
        home_queries = [lax.all_gather(plane_queries, "k", axis=0, tiled=False)]
    away_queries = [lax.ppermute(q, "core", swap) for q in home_queries]

    width = out_weight.shape[1] // head_axis
    held = [hold(device, out_weight, head_axis, own)] if head_axis == 2 else []
    away, home = (
        attend(some, kv, device, k, g_count, head_axis, (held + kv)[0])
        for some in (away_queries, home_queries)
    )
    away, home = (some.reshape(k * g_count, rows, -1) for some in (away, home))
    count = k * g_count
    part_turns = PART_TURNS if count == len(PART_TURNS) else tuple(range(count))
    arrived = lax.ppermute(away, "core", swap)
    part_turns = part_turns[SPLIT:] + part_turns[:SPLIT]
    last, first = (
        merge_pair(device, home, arrived, heads, some, g_count, head_axis)
        for some in (part_turns[:-SPLIT], part_turns[-SPLIT:])
    )
    parts = last + first
    parts = [
        lax.ppermute(part, ("k", "g"), [(i, i ^ d) for i in range(count)]) if d else part
        for d, part in zip(part_turns, parts)
    ]

    merged = (2 * rows, out_weight.shape[0])
    merging = functools.partial(first_kernel, heads, g_count, head_axis, part_turns, len(held))
    if head_axis == 2:
        first = width // 2
        sent, both = project(
            merging, device, parts, out_weight, first, jnp.bfloat16, merged, held
        )
        received = [lax.ppermute(sent, "head", swap)]
        (sent,) = project(
            rest_kernel, device, [both], out_weight, width - first, jnp.bfloat16, None, held
        )
        received.append(lax.ppermute(sent, "head", swap))
        own_half = functools.partial(second_kernel, head_axis)
        (own,) = project(own_half, device, [both], out_weight, width, jnp.float32)
        outs = ()
        for part, arrived in enumerate(received):
            outs = sum_columns(own, arrived, part, outs)
        return tuple(outs)
    else:
        partial, _ = project(
            merging, device, parts, out_weight, width * head_axis, jnp.float32, merged
        )
        total = lax.psum_scatter(partial, "head", scatter_dimension=1, tiled=True)
    total = total.astype(jnp.bfloat16)
    return (total[:rows], total[rows:])


def solution(mesh):
    blk, head_axis = mesh.shape["blk"], mesh.shape["head"]
    g_count = math.gcd(H // head_axis, blk // 2)
    fine = Mesh(
        mesh.devices.reshape(blk // (2 * g_count), g_count, 2, head_axis),
        ("k", "g", "core", "head"),
    )
    rows = P(("k", "g", "core", "head"), None)
    return jax.shard_map(
        local,
        mesh=fine,
        in_specs=(rows,) * 6 + (P("head", None),),
        out_specs=(P(("k", "g", "core"), "head"),) * 2,
        check_vma=False,
    )
```

```python
import functools
import math

import jax
import jax.numpy as jnp
from jax import lax
from jax.experimental import pallas as pl
from jax.experimental.pallas import tpu as pltpu
from jax.sharding import Mesh, PartitionSpec as P

H = 24
DH = 128
NT = (((1,), (1,)), ((), ()))
PART_TURNS = (4, 6, 5, 7, 1, 2, 3, 0)
SPLIT = 4
TURNS = (2, 1, 4)
FAR = 7
ATTEND_VMEM = 16 * 2**20
PROJECT_VMEM = 20 * 2**20


def position(device_ref, g_count, head_axis):
    device = device_ref[0]
    pair = 2 * head_axis
    return device // (pair * g_count), device // pair % g_count, device % head_axis


def split_bf16(x, parts):
    terms = []
    for _ in range(parts):
        term = x.astype(jnp.bfloat16)
        terms.append(term)
        x = x - term.astype(jnp.float32)
    return terms


def attend_kernel(heads, row_len, kv_count, device_ref, after_ref, *refs):
    query_refs, kv_refs, out_ref = refs[: -kv_count - 1], refs[-kv_count - 1 : -1], refs[-1]
    g_count, head_axis = out_ref.shape[1], out_ref.shape[2] // row_len
    plane_rows = g_count * head_axis * row_len
    scale = DH ** (-0.5)

    def some_planes(blocks, planes):
        rows = len(blocks) * plane_rows
        lane = lax.broadcasted_iota(jnp.int32, (rows, DH), 1)
        lse = slopes_mean = jnp.zeros((rows, DH), jnp.float32)

        def put(x, columns):
            for i, plane in enumerate(planes):
                for head in range(head_axis):
                    for g in range(g_count):
                        here = i * plane_rows + (head * g_count + g) * row_len
                        there = slice(head * row_len, (head + 1) * row_len)
                        out_ref[plane, g, there, columns] = x[here : here + row_len]

        for h in range(heads):
            lanes = slice(h * DH, (h + 1) * DH)
            key, key_tan, value, value_tan = (
                jnp.concatenate([ref[t, :, lanes] for ref in kv_refs]) for t in range(4)
            )
            query, qtan = (
                jnp.concatenate(
                    [ref[j, :, t, :, lanes].reshape(plane_rows, DH) for ref, j in blocks]
                )
                for t in range(2)
            )
            scores = lax.dot_general(query, key, NT, preferred_element_type=jnp.float32) * scale
            slopes = (
                lax.dot_general(
                    jnp.concatenate([qtan, query], axis=1),
                    jnp.concatenate([key, key_tan], axis=1),
                    NT,
                    preferred_element_type=jnp.float32,
                )
                * scale
            )
            peak = jnp.max(scores, axis=1, keepdims=True)
            unnormed = jnp.exp(scores - peak)
            tilted = unnormed * slopes
            total = jnp.sum(unnormed, axis=1, keepdims=True)
            slope_sum = jnp.sum(tilted, axis=1, keepdims=True)
            sums = jnp.dot(
                unnormed.astype(jnp.bfloat16),
                jnp.concatenate([value, value_tan], axis=1),
                preferred_element_type=jnp.float32,
            )
            tilted_sum = jnp.dot(
                tilted.astype(jnp.bfloat16), value, preferred_element_type=jnp.float32
            )
            inv = 1.0 / total
            mean_slope = slope_sum * inv
            mean_value = sums[:, :DH] * inv
            tangent = (sums[:, DH:] + tilted_sum) * inv - mean_slope * mean_value
            both = jnp.concatenate([mean_value, tangent], axis=1).astype(jnp.bfloat16)
            put(both, slice(2 * h * DH, 2 * (h + 1) * DH))
            lse = jnp.where(lane == h, peak + jnp.log(total), lse)
            slopes_mean = jnp.where(lane == h, mean_slope, slopes_mean)
        put(packed_stats(lse, slopes_mean, heads), slice(2 * heads * DH, (2 * heads + 1) * DH))

    if len(query_refs) > 1:
        k, _, _ = position(device_ref, g_count, head_axis)
        planes = [k ^ d for d in range(len(query_refs))]
        some_planes([(ref, 0) for ref in query_refs], planes)
    else:
        (ref,) = query_refs
        count = math.gcd(ref.shape[0], 4)

        @pl.loop(0, ref.shape[0] // count)
        def _(step):
            planes = [step * count + j for j in range(count)]
            some_planes([(ref, j) for j in planes], planes)


def attend(queries, kv, device, k, g_count, head_axis, after):
    heads = kv[0].shape[2] // DH
    row_len = queries[0].shape[3]
    out_shape = (k, g_count, head_axis * row_len, heads * 2 * DH + DH)
    whole = pl.BlockSpec(memory_space=pltpu.VMEM)
    return pl.pallas_call(
        functools.partial(attend_kernel, heads, row_len, len(kv)),
        out_shape=jax.ShapeDtypeStruct(out_shape, jnp.bfloat16),
        in_specs=[pl.BlockSpec(memory_space=pltpu.SMEM), pl.BlockSpec(memory_space=pl.ANY)]
        + [whole] * (len(queries) + len(kv)),
        out_specs=whole,
        compiler_params=pltpu.CompilerParams(vmem_limit_bytes=ATTEND_VMEM),
        name="attend",
    )(device, after, *queries, *kv)


def packed_stats(lse, slope, heads):
    lane = lax.broadcasted_iota(jnp.int32, lse.shape, 1)
    total = 0.0
    terms = split_bf16(jnp.where(lane < heads, lse, 0.0), 3)
    terms += split_bf16(jnp.where(lane < heads, slope, 0.0), 2)
    for i, term in enumerate(terms):
        term = term.astype(jnp.float32)
        total += pltpu.roll(term, i * heads, 1) if i else term
    return total.astype(jnp.bfloat16)


def merge_stats(tails, heads):
    def term(tail, i):
        return pltpu.roll(tail, DH - i * heads, 1) if i else tail

    tails = [tail.astype(jnp.float32) for tail in tails]
    lse = [term(tail, 0) + term(tail, 1) + term(tail, 2) for tail in tails]
    slope = [term(tail, 3) + term(tail, 4) for tail in tails]
    top = functools.reduce(jnp.maximum, lse)
    share = [jnp.exp(e - top) for e in lse]
    total = sum(share)
    inv = 1.0 / total
    share = [e * inv for e in share]
    mean_slope = sum(e * s for e, s in zip(share, slope))
    shift = [e * (s - mean_slope) for e, s in zip(share, slope)]
    return share, shift, top + jnp.log(total), mean_slope


def merge_head(owns, tans, share, shift, h):
    value = tangent = 0.0
    for own, own_tan, e, s in zip(owns, tans, share, shift):
        own, own_tan = own.astype(jnp.float32), own_tan.astype(jnp.float32)
        e, s = e[:, h : h + 1], s[:, h : h + 1]
        value += e * own
        tangent += e * own_tan + s * own
    return value, tangent


def merge(my_g, parts_refs, both_ref, heads, g_count, turns):
    rows = both_ref.shape[0] // 2
    tail = slice(2 * heads * DH, (2 * heads + 1) * DH)
    for d in range(g_count):
        g = my_g ^ d
        parts = [parts_refs[turns.index(j)] for j in range(d, len(turns), g_count)]
        tails = [part[2 * heads * rows :].astype(jnp.float32) for part in parts]
        tails = [jnp.concatenate([tail, pltpu.roll(tail, DH // 2, 1)]) for tail in tails]
        share, shift, _, _ = merge_stats(tails, heads)
        for h in range(heads):
            owns, tans = (
                [part[i * rows : (i + 1) * rows] for part in parts]
                for i in (2 * h, 2 * h + 1)
            )
            value, tangent = merge_head(owns, tans, share, shift, h)
            columns = pl.ds(pl.multiple_of((g * heads + h) * DH, DH), DH)
            both_ref[:rows, columns] = value.astype(jnp.bfloat16)
            both_ref[rows:, columns] = tangent.astype(jnp.bfloat16)


def pair_kernel(heads, turns, g_count, head_axis, device_ref, home_ref, away_ref, *out_refs):
    k, g, _ = position(device_ref, g_count, head_axis)
    tail = slice(2 * heads * DH, (2 * heads + 1) * DH)
    for d, out_ref in zip(turns, out_refs):
        parts = [ref[(k * g_count + g) ^ d] for ref in (home_ref, away_ref)]
        rows = parts[0].shape[0]
        share, shift, lse, slope = merge_stats([part[:, tail] for part in parts], heads)
        for h in range(heads):
            owns, tans = (
                [part[:, i * DH : (i + 1) * DH] for part in parts] for i in (2 * h, 2 * h + 1)
            )
            for i, x in enumerate(merge_head(owns, tans, share, shift, h)):
                first = (2 * h + i) * rows
                out_ref[first : first + rows] = x.astype(jnp.bfloat16)
        packed = packed_stats(lse, slope, heads).astype(jnp.float32)
        packed = packed[: rows // 2] + pltpu.roll(packed[rows // 2 :], DH // 2, 1)
        out_ref[2 * heads * rows :] = packed.astype(jnp.bfloat16)


def merge_pair(device, home, away, heads, turns, g_count, head_axis):
    whole = pl.BlockSpec(memory_space=pltpu.VMEM)
    count = len(turns)
    rows = home.shape[1]
    size = 2 * heads * rows + rows // 2
    return pl.pallas_call(
        functools.partial(pair_kernel, heads, turns, g_count, head_axis),
        out_shape=[jax.ShapeDtypeStruct((size, DH), home.dtype)] * count,
        in_specs=[pl.BlockSpec(memory_space=pltpu.SMEM), whole, whole],
        out_specs=[whole] * count,
        compiler_params=pltpu.CompilerParams(vmem_limit_bytes=ATTEND_VMEM),
        name="merge_pair",
    )(device, home, away)


def first_kernel(heads, g_count, head_axis, turns, held_count, device_ref, weight_ref, *refs):
    _, my_g, _ = position(device_ref, g_count, head_axis)
    if held_count:
        *refs, out_ref, both_ref = refs
        parts_refs, held_refs = refs[:-held_count], refs[-held_count:]
        merge(my_g, parts_refs, both_ref, heads, g_count, turns)
        for held in held_refs:
            times(both_ref, held[:, : out_ref.shape[1]], out_ref, 0)
    else:
        *parts_refs, out_ref, both_ref, held, sems = refs
        copies = fetch(0, weight_ref, held, sems)
        merge(my_g, parts_refs, both_ref, heads, g_count, turns)
        times_held(copies, both_ref, out_ref, held)


def times(both_ref, columns, out_ref, i):
    tile = columns.shape[1]
    out_ref[:, i * tile : (i + 1) * tile] = jnp.dot(
        both_ref[...], columns, preferred_element_type=jnp.float32
    ).astype(out_ref.dtype)


def rest_kernel(device_ref, weight_ref, both_ref, held_ref, out_ref):
    times(both_ref, held_ref[:, held_ref.shape[1] - out_ref.shape[1] :], out_ref, 0)


def sum_kernel(own_ref, received_ref, *refs):
    rows = own_ref.shape[0] // 2
    total = (own_ref[...] + received_ref[...].astype(jnp.float32)).astype(jnp.bfloat16)
    refs[-2][...] = total[:rows]
    refs[-1][...] = total[rows:]


def sum_columns(own, received, part, outs=()):
    rows, tile = own.shape[0] // 2, received.shape[1]
    shape = jax.ShapeDtypeStruct((rows, own.shape[1]), jnp.bfloat16)
    return pl.pallas_call(
        sum_kernel,
        grid=(1,),
        out_shape=[shape] * 2,
        in_specs=[
            pl.BlockSpec((2 * rows, tile), lambda n: (0, part)),
            pl.BlockSpec((2 * rows, tile), lambda n: (0, 0)),
        ]
        + [pl.BlockSpec(memory_space=pl.ANY)] * len(outs),
        out_specs=[pl.BlockSpec((rows, tile), lambda n: (0, part))] * 2,
        input_output_aliases={2 + i: i for i in range(len(outs))},
        compiler_params=pltpu.CompilerParams(vmem_limit_bytes=8 * 2**20),
        name="sum_columns",
    )(own, received, *outs)


def second_kernel(head_axis, device_ref, weight_ref, both_ref, out_ref, held, sems):
    _, _, head = position(device_ref, 1, head_axis)
    times_held(fetch(head, weight_ref, held, sems), both_ref, out_ref, held)


def fetch(half, weight_ref, held, sems):
    chunks, _, tile = held.shape
    copies = []
    for i in range(chunks):
        first = pl.multiple_of((half * chunks + i) * tile, tile)
        copy = pltpu.make_async_copy(weight_ref.at[:, pl.ds(first, tile)], held.at[i], sems.at[i])
        copy.start()
        copies.append(copy)
    return copies


def times_held(copies, both_ref, out_ref, held):
    for i, copy in enumerate(copies):
        copy.wait()
        times(both_ref, held[i], out_ref, i)


def project(kernel, device, left, weight, width, dtype, merged=None, held=()):
    depth = weight.shape[0]
    chunks = 4
    rows = merged[0] if merged else left[0].shape[0]
    outs = [jax.ShapeDtypeStruct((rows, width), dtype)]
    if merged:
        outs.append(jax.ShapeDtypeStruct(merged, jnp.bfloat16))
    whole = pl.BlockSpec(memory_space=pltpu.VMEM)
    scalar = pl.BlockSpec(memory_space=pltpu.SMEM)
    scratch = [
        pltpu.VMEM((chunks, depth, width // chunks), jnp.bfloat16),
        pltpu.SemaphoreType.DMA((chunks,)),
    ]
    if held:
        scratch = []
    return pl.pallas_call(
        kernel,
        out_shape=outs,
        in_specs=[scalar, pl.BlockSpec(memory_space=pl.ANY)] + [whole] * (len(left) + len(held)),
        out_specs=[whole] * len(outs),
        scratch_shapes=scratch,
        compiler_params=pltpu.CompilerParams(vmem_limit_bytes=PROJECT_VMEM),
        cost_estimate=pl.CostEstimate(
            flops=2 * rows * depth * width, bytes_accessed=2 * depth * width, transcendentals=0
        ),
        name="project",
    )(device, pltpu.with_memory_space_constraint(weight, pltpu.HBM), *left, *held)


def pack_kernel(g_count, head_axis, device_ref, *refs):
    matrix_refs, (query_ref, own_ref, far_ref, mine_ref, other_ref) = refs[:6], refs[6:11]
    held_refs, sems = refs[11:-1], refs[-1]
    width = query_ref.shape[3]
    _, g, head = position(device_ref, g_count, head_axis)
    core = device_ref[0] // head_axis % 2
    copies = [
        pltpu.make_async_copy(ref, held, sems.at[i])
        for i, (ref, held) in enumerate(zip(matrix_refs, held_refs))
    ]
    for copy in copies:
        copy.start()
    for t in range(2):
        copies[t].wait()
        for i in range(query_ref.shape[0]):
            query_ref[i, t] = held_refs[t][:, i * width : (i + 1) * width]
    for t in range(4):
        copies[2 + t].wait()

        def piece(turn):
            partner = (g * head_axis + head) ^ turn
            column = (partner % head_axis) * g_count + partner // head_axis
            return held_refs[2 + t][:, pl.ds(pl.multiple_of(column * width, width), width)]

        own_ref[t] = piece(0)
        far_ref[t] = piece(FAR)
        for j, turn in enumerate(TURNS):
            mine_ref[j, t] = piece(turn ^ (FAR * core))
            other_ref[j, t] = piece(turn ^ (FAR * (1 - core)))


def pack(group, g_count, head_axis, device, *matrices):
    rows, columns = matrices[0].shape
    width = columns // group
    piece = (4, matrices[2].shape[0], width)
    shapes = [(group, 2, rows, width), piece, piece] + [(len(TURNS),) + piece] * 2
    return pl.pallas_call(
        functools.partial(pack_kernel, g_count, head_axis),
        out_shape=[jax.ShapeDtypeStruct(shape, jnp.bfloat16) for shape in shapes],
        in_specs=[pl.BlockSpec(memory_space=pltpu.SMEM)]
        + [pl.BlockSpec(memory_space=pl.ANY)] * len(matrices),
        out_specs=[pl.BlockSpec(memory_space=pltpu.VMEM)] * len(shapes),
        scratch_shapes=[pltpu.VMEM(m.shape, m.dtype) for m in matrices]
        + [pltpu.SemaphoreType.DMA((len(matrices),))],
        compiler_params=pltpu.CompilerParams(vmem_limit_bytes=8 * 2**20),
        name="pack",
    )(device, *(pltpu.with_memory_space_constraint(m, pltpu.HBM) for m in matrices))


def join_kernel(mine_ref, theirs_ref, *out_refs):
    rows = mine_ref.shape[2]
    for j, out_ref in enumerate(out_refs):
        out_ref[:, :rows] = mine_ref[j]
        out_ref[:, rows:] = theirs_ref[j]


def join(mine, theirs):
    count, tensors, rows, width = mine.shape
    whole = pl.BlockSpec(memory_space=pltpu.VMEM)
    return pl.pallas_call(
        join_kernel,
        out_shape=[jax.ShapeDtypeStruct((tensors, 2 * rows, width), mine.dtype)] * count,
        in_specs=[whole, whole],
        out_specs=[whole] * count,
        compiler_params=pltpu.CompilerParams(vmem_limit_bytes=8 * 2**20),
        name="join",
    )(mine, theirs)


def across_chips(turn, g_count, head_axis):
    pairs = []
    for n in range(g_count * head_axis):
        for core in range(2):
            m = n ^ turn ^ (FAR * core)
            number = [(i // head_axis * 2 + core) * head_axis + i % head_axis for i in (n, m)]
            pairs.append(tuple(number))
    return pairs


def hold_kernel(head_axis, device_ref, weight_ref, after_ref, out_ref, sems):
    count = sems.shape[0]
    rows, width = out_ref.shape[0] // count, out_ref.shape[1]
    _, _, head = position(device_ref, 1, head_axis)
    columns = pl.ds(pl.multiple_of((1 - head) * width, width), width)
    copies = [
        pltpu.make_async_copy(
            weight_ref.at[pl.ds(i * rows, rows), columns],
            out_ref.at[pl.ds(i * rows, rows)],
            sems.at[i],
        )
        for i in range(count)
    ]
    for copy in copies:
        copy.start()
    for copy in copies:
        copy.wait()


def hold(device, weight, head_axis, after):
    anywhere = pl.BlockSpec(memory_space=pl.ANY)
    width = weight.shape[1] // head_axis
    size = weight.shape[0] * width
    return pl.pallas_call(
        functools.partial(hold_kernel, head_axis),
        out_shape=jax.ShapeDtypeStruct((weight.shape[0], width), weight.dtype),
        in_specs=[pl.BlockSpec(memory_space=pltpu.SMEM), anywhere, anywhere],
        out_specs=pl.BlockSpec(memory_space=pltpu.VMEM),
        scratch_shapes=[pltpu.SemaphoreType.DMA((8,))],
        compiler_params=pltpu.CompilerParams(vmem_limit_bytes=12 * 2**20),
        cost_estimate=pl.CostEstimate(flops=0, bytes_accessed=2 * size, transcendentals=0),
        name="hold",
    )(device, pltpu.with_memory_space_constraint(weight, pltpu.HBM), after)


def local(queries, query_tangent, key_rows, key_tangent, value_rows, value_tangent, out_weight):
    k, g_count, head_axis = (lax.axis_size(a) for a in ("k", "g", "head"))
    plane_axes = ("head", "g")
    group = g_count * head_axis
    heads = H // group
    rows = queries.shape[0] * head_axis
    swap = [(0, 1), (1, 0)]

    def within_plane(x):
        return lax.all_to_all(x, plane_axes, split_axis=0, concat_axis=0, tiled=True)

    device = lax.axis_index(("k", "g", "core", "head")).astype(jnp.int32).reshape(1)
    packed_queries, own, far, mine, other = pack(
        group,
        g_count,
        head_axis,
        device,
        queries,
        query_tangent,
        key_rows,
        key_tangent,
        value_rows,
        value_tangent,
    )
    plane_queries = within_plane(packed_queries)
    pieces = join(mine, lax.ppermute(other, "core", swap))
    kv = [own]
    kv += [
        lax.ppermute(piece, ("g", "core", "head"), across_chips(turn, g_count, head_axis))
        for turn, piece in zip(TURNS, pieces)
    ]
    kv.append(lax.ppermute(far, ("g", "head"), [(i, i ^ FAR) for i in range(group)]))
    if k == 2:
        home_queries = [plane_queries[None], lax.ppermute(plane_queries, "k", swap)[None]]
    else:
        home_queries = [lax.all_gather(plane_queries, "k", axis=0, tiled=False)]
    away_queries = [lax.ppermute(q, "core", swap) for q in home_queries]

    width = out_weight.shape[1] // head_axis
    held = [hold(device, out_weight, head_axis, own)] if head_axis == 2 else []
    away, home = (
        attend(some, kv, device, k, g_count, head_axis, (held + kv)[0])
        for some in (away_queries, home_queries)
    )
    away, home = (some.reshape(k * g_count, rows, -1) for some in (away, home))
    count = k * g_count
    part_turns = PART_TURNS if count == len(PART_TURNS) else tuple(range(count))
    arrived = lax.ppermute(away, "core", swap)
    part_turns = part_turns[SPLIT:] + part_turns[:SPLIT]
    last, first = (
        merge_pair(device, home, arrived, heads, some, g_count, head_axis)
        for some in (part_turns[:-SPLIT], part_turns[-SPLIT:])
    )
    parts = last + first
    parts = [
        lax.ppermute(part, ("k", "g"), [(i, i ^ d) for i in range(count)]) if d else part
        for d, part in zip(part_turns, parts)
    ]

    merged = (2 * rows, out_weight.shape[0])
    merging = functools.partial(first_kernel, heads, g_count, head_axis, part_turns, len(held))
    if head_axis == 2:
        first = width // 2
        sent, both = project(
            merging, device, parts, out_weight, first, jnp.bfloat16, merged, held
        )
        received = [lax.ppermute(sent, "head", swap)]
        (sent,) = project(
            rest_kernel, device, [both], out_weight, width - first, jnp.bfloat16, None, held
        )
        received.append(lax.ppermute(sent, "head", swap))
        own_half = functools.partial(second_kernel, head_axis)
        (own,) = project(own_half, device, [both], out_weight, width, jnp.float32)
        outs = ()
        for part, arrived in enumerate(received):
            outs = sum_columns(own, arrived, part, outs)
        return tuple(outs)
    else:
        partial, _ = project(
            merging, device, parts, out_weight, width * head_axis, jnp.float32, merged
        )
        total = lax.psum_scatter(partial, "head", scatter_dimension=1, tiled=True)
    total = total.astype(jnp.bfloat16)
    return (total[:rows], total[rows:])


def solution(mesh):
    blk, head_axis = mesh.shape["blk"], mesh.shape["head"]
    g_count = math.gcd(H // head_axis, blk // 2)
    fine = Mesh(
        mesh.devices.reshape(blk // (2 * g_count), g_count, 2, head_axis),
        ("k", "g", "core", "head"),
    )
    rows = P(("k", "g", "core", "head"), None)
    return jax.shard_map(
        local,
        mesh=fine,
        in_specs=(rows,) * 6 + (P("head", None),),
        out_specs=(P(("k", "g", "core"), "head"),) * 2,
        check_vma=False,
    )
```

```python
import functools
import math

import jax
import jax.numpy as jnp
from jax import lax
from jax.experimental import pallas as pl
from jax.experimental.pallas import tpu as pltpu
from jax.sharding import Mesh, PartitionSpec as P

H = 24
DH = 128
NT = (((1,), (1,)), ((), ()))
PART_TURNS = (4, 5, 6, 7, 2, 1, 3, 0)
SPLIT = 4
TURNS = (2, 1, 4)
FAR = 7
ATTEND_VMEM = 16 * 2**20
PROJECT_VMEM = 20 * 2**20


def position(device_ref, g_count, head_axis):
    device = device_ref[0]
    pair = 2 * head_axis
    return device // (pair * g_count), device // pair % g_count, device % head_axis


def split_bf16(x, parts):
    terms = []
    for _ in range(parts):
        term = x.astype(jnp.bfloat16)
        terms.append(term)
        x = x - term.astype(jnp.float32)
    return terms


def attend_kernel(heads, row_len, kv_count, device_ref, after_ref, *refs):
    query_refs, kv_refs, out_ref = refs[: -kv_count - 1], refs[-kv_count - 1 : -1], refs[-1]
    g_count, head_axis = out_ref.shape[1], out_ref.shape[2] // row_len
    plane_rows = g_count * head_axis * row_len
    scale = DH ** (-0.5)

    def some_planes(blocks, planes):
        rows = len(blocks) * plane_rows
        lane = lax.broadcasted_iota(jnp.int32, (rows, DH), 1)
        lse = slopes_mean = jnp.zeros((rows, DH), jnp.float32)

        def put(x, columns):
            for i, plane in enumerate(planes):
                for head in range(head_axis):
                    for g in range(g_count):
                        here = i * plane_rows + (head * g_count + g) * row_len
                        there = slice(head * row_len, (head + 1) * row_len)
                        out_ref[plane, g, there, columns] = x[here : here + row_len]

        for h in range(heads):
            lanes = slice(h * DH, (h + 1) * DH)
            key, key_tan, value, value_tan = (
                jnp.concatenate([ref[t, :, lanes] for ref in kv_refs]) for t in range(4)
            )
            query, qtan = (
                jnp.concatenate(
                    [ref[j, :, t, :, lanes].reshape(plane_rows, DH) for ref, j in blocks]
                )
                for t in range(2)
            )
            scores = lax.dot_general(query, key, NT, preferred_element_type=jnp.float32) * scale
            slopes = (
                lax.dot_general(
                    jnp.concatenate([qtan, query], axis=1),
                    jnp.concatenate([key, key_tan], axis=1),
                    NT,
                    preferred_element_type=jnp.float32,
                )
                * scale
            )
            peak = jnp.max(scores, axis=1, keepdims=True)
            unnormed = jnp.exp(scores - peak)
            tilted = unnormed * slopes
            total = jnp.sum(unnormed, axis=1, keepdims=True)
            slope_sum = jnp.sum(tilted, axis=1, keepdims=True)
            sums = jnp.dot(
                unnormed.astype(jnp.bfloat16),
                jnp.concatenate([value, value_tan], axis=1),
                preferred_element_type=jnp.float32,
            )
            tilted_sum = jnp.dot(
                tilted.astype(jnp.bfloat16), value, preferred_element_type=jnp.float32
            )
            inv = 1.0 / total
            mean_slope = slope_sum * inv
            mean_value = sums[:, :DH] * inv
            tangent = (sums[:, DH:] + tilted_sum) * inv - mean_slope * mean_value
            both = jnp.concatenate([mean_value, tangent], axis=1).astype(jnp.bfloat16)
            put(both, slice(2 * h * DH, 2 * (h + 1) * DH))
            lse = jnp.where(lane == h, peak + jnp.log(total), lse)
            slopes_mean = jnp.where(lane == h, mean_slope, slopes_mean)
        put(packed_stats(lse, slopes_mean, heads), slice(2 * heads * DH, (2 * heads + 1) * DH))

    if len(query_refs) > 1:
        k, _, _ = position(device_ref, g_count, head_axis)
        planes = [k ^ d for d in range(len(query_refs))]
        some_planes([(ref, 0) for ref in query_refs], planes)
    else:
        (ref,) = query_refs
        count = math.gcd(ref.shape[0], 4)

        @pl.loop(0, ref.shape[0] // count)
        def _(step):
            planes = [step * count + j for j in range(count)]
            some_planes([(ref, j) for j in planes], planes)


def attend(queries, kv, device, k, g_count, head_axis, after):
    heads = kv[0].shape[2] // DH
    row_len = queries[0].shape[3]
    out_shape = (k, g_count, head_axis * row_len, heads * 2 * DH + DH)
    whole = pl.BlockSpec(memory_space=pltpu.VMEM)
    return pl.pallas_call(
        functools.partial(attend_kernel, heads, row_len, len(kv)),
        out_shape=jax.ShapeDtypeStruct(out_shape, jnp.bfloat16),
        in_specs=[pl.BlockSpec(memory_space=pltpu.SMEM), pl.BlockSpec(memory_space=pl.ANY)]
        + [whole] * (len(queries) + len(kv)),
        out_specs=whole,
        compiler_params=pltpu.CompilerParams(vmem_limit_bytes=ATTEND_VMEM),
        name="attend",
    )(device, after, *queries, *kv)


def packed_stats(lse, slope, heads):
    lane = lax.broadcasted_iota(jnp.int32, lse.shape, 1)
    total = 0.0
    terms = split_bf16(jnp.where(lane < heads, lse, 0.0), 3)
    terms += split_bf16(jnp.where(lane < heads, slope, 0.0), 2)
    for i, term in enumerate(terms):
        term = term.astype(jnp.float32)
        total += pltpu.roll(term, i * heads, 1) if i else term
    return total.astype(jnp.bfloat16)


def merge_stats(tails, heads):
    def term(tail, i):
        return pltpu.roll(tail, DH - i * heads, 1) if i else tail

    tails = [tail.astype(jnp.float32) for tail in tails]
    lse = [term(tail, 0) + term(tail, 1) + term(tail, 2) for tail in tails]
    slope = [term(tail, 3) + term(tail, 4) for tail in tails]
    top = functools.reduce(jnp.maximum, lse)
    share = [jnp.exp(e - top) for e in lse]
    total = sum(share)
    inv = 1.0 / total
    share = [e * inv for e in share]
    mean_slope = sum(e * s for e, s in zip(share, slope))
    shift = [e * (s - mean_slope) for e, s in zip(share, slope)]
    return share, shift, top + jnp.log(total), mean_slope


def merge_head(owns, tans, share, shift, h):
    value = tangent = 0.0
    for own, own_tan, e, s in zip(owns, tans, share, shift):
        own, own_tan = own.astype(jnp.float32), own_tan.astype(jnp.float32)
        e, s = e[:, h : h + 1], s[:, h : h + 1]
        value += e * own
        tangent += e * own_tan + s * own
    return value, tangent


def merge(my_g, parts_refs, both_ref, heads, g_count, turns):
    rows = both_ref.shape[0] // 2
    tail = slice(2 * heads * DH, (2 * heads + 1) * DH)
    for d in range(g_count):
        g = my_g ^ d
        parts = [parts_refs[turns.index(j)] for j in range(d, len(turns), g_count)]
        tails = [part[2 * heads * rows :].astype(jnp.float32) for part in parts]
        tails = [jnp.concatenate([tail, pltpu.roll(tail, DH // 2, 1)]) for tail in tails]
        share, shift, _, _ = merge_stats(tails, heads)
        for h in range(heads):
            owns, tans = (
                [part[i * rows : (i + 1) * rows] for part in parts]
                for i in (2 * h, 2 * h + 1)
            )
            value, tangent = merge_head(owns, tans, share, shift, h)
            columns = pl.ds(pl.multiple_of((g * heads + h) * DH, DH), DH)
            both_ref[:rows, columns] = value.astype(jnp.bfloat16)
            both_ref[rows:, columns] = tangent.astype(jnp.bfloat16)


def pair_kernel(heads, turns, g_count, head_axis, device_ref, home_ref, away_ref, *out_refs):
    k, g, _ = position(device_ref, g_count, head_axis)
    tail = slice(2 * heads * DH, (2 * heads + 1) * DH)
    for d, out_ref in zip(turns, out_refs):
        parts = [ref[(k * g_count + g) ^ d] for ref in (home_ref, away_ref)]
        rows = parts[0].shape[0]
        share, shift, lse, slope = merge_stats([part[:, tail] for part in parts], heads)
        for h in range(heads):
            owns, tans = (
                [part[:, i * DH : (i + 1) * DH] for part in parts] for i in (2 * h, 2 * h + 1)
            )
            for i, x in enumerate(merge_head(owns, tans, share, shift, h)):
                first = (2 * h + i) * rows
                out_ref[first : first + rows] = x.astype(jnp.bfloat16)
        packed = packed_stats(lse, slope, heads).astype(jnp.float32)
        packed = packed[: rows // 2] + pltpu.roll(packed[rows // 2 :], DH // 2, 1)
        out_ref[2 * heads * rows :] = packed.astype(jnp.bfloat16)


def merge_pair(device, home, away, heads, turns, g_count, head_axis):
    whole = pl.BlockSpec(memory_space=pltpu.VMEM)
    count = len(turns)
    rows = home.shape[1]
    size = 2 * heads * rows + rows // 2
    return pl.pallas_call(
        functools.partial(pair_kernel, heads, turns, g_count, head_axis),
        out_shape=[jax.ShapeDtypeStruct((size, DH), home.dtype)] * count,
        in_specs=[pl.BlockSpec(memory_space=pltpu.SMEM), whole, whole],
        out_specs=[whole] * count,
        compiler_params=pltpu.CompilerParams(vmem_limit_bytes=ATTEND_VMEM),
        name="merge_pair",
    )(device, home, away)


def first_kernel(heads, g_count, head_axis, turns, held_count, device_ref, weight_ref, *refs):
    _, my_g, _ = position(device_ref, g_count, head_axis)
    if held_count:
        *refs, out_ref, both_ref = refs
        parts_refs, held_refs = refs[:-held_count], refs[-held_count:]
        merge(my_g, parts_refs, both_ref, heads, g_count, turns)
        for held in held_refs:
            times(both_ref, held[:, : out_ref.shape[1]], out_ref, 0)
    else:
        *parts_refs, out_ref, both_ref, held, sems = refs
        copies = fetch(0, weight_ref, held, sems)
        merge(my_g, parts_refs, both_ref, heads, g_count, turns)
        times_held(copies, both_ref, out_ref, held)


def times(both_ref, columns, out_ref, i):
    tile = columns.shape[1]
    out_ref[:, i * tile : (i + 1) * tile] = jnp.dot(
        both_ref[...], columns, preferred_element_type=jnp.float32
    ).astype(out_ref.dtype)


def rest_kernel(device_ref, weight_ref, both_ref, held_ref, out_ref):
    times(both_ref, held_ref[:, held_ref.shape[1] - out_ref.shape[1] :], out_ref, 0)


def sum_kernel(own_ref, received_ref, *refs):
    rows = own_ref.shape[0] // 2
    total = (own_ref[...] + received_ref[...].astype(jnp.float32)).astype(jnp.bfloat16)
    refs[-2][...] = total[:rows]
    refs[-1][...] = total[rows:]


def sum_columns(own, received, part, outs=()):
    rows, tile = own.shape[0] // 2, received.shape[1]
    shape = jax.ShapeDtypeStruct((rows, own.shape[1]), jnp.bfloat16)
    return pl.pallas_call(
        sum_kernel,
        grid=(1,),
        out_shape=[shape] * 2,
        in_specs=[
            pl.BlockSpec((2 * rows, tile), lambda n: (0, part)),
            pl.BlockSpec((2 * rows, tile), lambda n: (0, 0)),
        ]
        + [pl.BlockSpec(memory_space=pl.ANY)] * len(outs),
        out_specs=[pl.BlockSpec((rows, tile), lambda n: (0, part))] * 2,
        input_output_aliases={2 + i: i for i in range(len(outs))},
        compiler_params=pltpu.CompilerParams(vmem_limit_bytes=8 * 2**20),
        name="sum_columns",
    )(own, received, *outs)


def second_kernel(head_axis, device_ref, weight_ref, both_ref, out_ref, held, sems):
    _, _, head = position(device_ref, 1, head_axis)
    times_held(fetch(head, weight_ref, held, sems), both_ref, out_ref, held)


def fetch(half, weight_ref, held, sems):
    chunks, _, tile = held.shape
    copies = []
    for i in range(chunks):
        first = pl.multiple_of((half * chunks + i) * tile, tile)
        copy = pltpu.make_async_copy(weight_ref.at[:, pl.ds(first, tile)], held.at[i], sems.at[i])
        copy.start()
        copies.append(copy)
    return copies


def times_held(copies, both_ref, out_ref, held):
    for i, copy in enumerate(copies):
        copy.wait()
        times(both_ref, held[i], out_ref, i)


def project(kernel, device, left, weight, width, dtype, merged=None, held=()):
    depth = weight.shape[0]
    chunks = 4
    rows = merged[0] if merged else left[0].shape[0]
    outs = [jax.ShapeDtypeStruct((rows, width), dtype)]
    if merged:
        outs.append(jax.ShapeDtypeStruct(merged, jnp.bfloat16))
    whole = pl.BlockSpec(memory_space=pltpu.VMEM)
    scalar = pl.BlockSpec(memory_space=pltpu.SMEM)
    scratch = [
        pltpu.VMEM((chunks, depth, width // chunks), jnp.bfloat16),
        pltpu.SemaphoreType.DMA((chunks,)),
    ]
    if held:
        scratch = []
    return pl.pallas_call(
        kernel,
        out_shape=outs,
        in_specs=[scalar, pl.BlockSpec(memory_space=pl.ANY)] + [whole] * (len(left) + len(held)),
        out_specs=[whole] * len(outs),
        scratch_shapes=scratch,
        compiler_params=pltpu.CompilerParams(vmem_limit_bytes=PROJECT_VMEM),
        cost_estimate=pl.CostEstimate(
            flops=2 * rows * depth * width, bytes_accessed=2 * depth * width, transcendentals=0
        ),
        name="project",
    )(device, pltpu.with_memory_space_constraint(weight, pltpu.HBM), *left, *held)


def pack_kernel(g_count, head_axis, device_ref, *refs):
    matrix_refs, (query_ref, own_ref, far_ref, mine_ref, other_ref) = refs[:6], refs[6:11]
    held_refs, sems = refs[11:-1], refs[-1]
    width = query_ref.shape[3]
    _, g, head = position(device_ref, g_count, head_axis)
    core = device_ref[0] // head_axis % 2
    copies = [
        pltpu.make_async_copy(ref, held, sems.at[i])
        for i, (ref, held) in enumerate(zip(matrix_refs, held_refs))
    ]
    for copy in copies:
        copy.start()
    for t in range(2):
        copies[t].wait()
        for i in range(query_ref.shape[0]):
            query_ref[i, t] = held_refs[t][:, i * width : (i + 1) * width]
    for t in range(4):
        copies[2 + t].wait()

        def piece(turn):
            partner = (g * head_axis + head) ^ turn
            column = (partner % head_axis) * g_count + partner // head_axis
            return held_refs[2 + t][:, pl.ds(pl.multiple_of(column * width, width), width)]

        own_ref[t] = piece(0)
        far_ref[t] = piece(FAR)
        for j, turn in enumerate(TURNS):
            mine_ref[j, t] = piece(turn ^ (FAR * core))
            other_ref[j, t] = piece(turn ^ (FAR * (1 - core)))


def pack(group, g_count, head_axis, device, *matrices):
    rows, columns = matrices[0].shape
    width = columns // group
    piece = (4, matrices[2].shape[0], width)
    shapes = [(group, 2, rows, width), piece, piece] + [(len(TURNS),) + piece] * 2
    return pl.pallas_call(
        functools.partial(pack_kernel, g_count, head_axis),
        out_shape=[jax.ShapeDtypeStruct(shape, jnp.bfloat16) for shape in shapes],
        in_specs=[pl.BlockSpec(memory_space=pltpu.SMEM)]
        + [pl.BlockSpec(memory_space=pl.ANY)] * len(matrices),
        out_specs=[pl.BlockSpec(memory_space=pltpu.VMEM)] * len(shapes),
        scratch_shapes=[pltpu.VMEM(m.shape, m.dtype) for m in matrices]
        + [pltpu.SemaphoreType.DMA((len(matrices),))],
        compiler_params=pltpu.CompilerParams(vmem_limit_bytes=8 * 2**20),
        name="pack",
    )(device, *(pltpu.with_memory_space_constraint(m, pltpu.HBM) for m in matrices))


def join_kernel(mine_ref, theirs_ref, *out_refs):
    rows = mine_ref.shape[2]
    for j, out_ref in enumerate(out_refs):
        out_ref[:, :rows] = mine_ref[j]
        out_ref[:, rows:] = theirs_ref[j]


def join(mine, theirs):
    count, tensors, rows, width = mine.shape
    whole = pl.BlockSpec(memory_space=pltpu.VMEM)
    return pl.pallas_call(
        join_kernel,
        out_shape=[jax.ShapeDtypeStruct((tensors, 2 * rows, width), mine.dtype)] * count,
        in_specs=[whole, whole],
        out_specs=[whole] * count,
        compiler_params=pltpu.CompilerParams(vmem_limit_bytes=8 * 2**20),
        name="join",
    )(mine, theirs)


def across_chips(turn, g_count, head_axis):
    pairs = []
    for n in range(g_count * head_axis):
        for core in range(2):
            m = n ^ turn ^ (FAR * core)
            number = [(i // head_axis * 2 + core) * head_axis + i % head_axis for i in (n, m)]
            pairs.append(tuple(number))
    return pairs


def hold_kernel(head_axis, device_ref, weight_ref, after_ref, out_ref, sems):
    count = sems.shape[0]
    rows, width = out_ref.shape[0] // count, out_ref.shape[1]
    _, _, head = position(device_ref, 1, head_axis)
    columns = pl.ds(pl.multiple_of((1 - head) * width, width), width)
    copies = [
        pltpu.make_async_copy(
            weight_ref.at[pl.ds(i * rows, rows), columns],
            out_ref.at[pl.ds(i * rows, rows)],
            sems.at[i],
        )
        for i in range(count)
    ]
    for copy in copies:
        copy.start()
    for copy in copies:
        copy.wait()


def hold(device, weight, head_axis, after):
    anywhere = pl.BlockSpec(memory_space=pl.ANY)
    width = weight.shape[1] // head_axis
    size = weight.shape[0] * width
    return pl.pallas_call(
        functools.partial(hold_kernel, head_axis),
        out_shape=jax.ShapeDtypeStruct((weight.shape[0], width), weight.dtype),
        in_specs=[pl.BlockSpec(memory_space=pltpu.SMEM), anywhere, anywhere],
        out_specs=pl.BlockSpec(memory_space=pltpu.VMEM),
        scratch_shapes=[pltpu.SemaphoreType.DMA((8,))],
        compiler_params=pltpu.CompilerParams(vmem_limit_bytes=12 * 2**20),
        cost_estimate=pl.CostEstimate(flops=0, bytes_accessed=2 * size, transcendentals=0),
        name="hold",
    )(device, pltpu.with_memory_space_constraint(weight, pltpu.HBM), after)


def local(queries, query_tangent, key_rows, key_tangent, value_rows, value_tangent, out_weight):
    k, g_count, head_axis = (lax.axis_size(a) for a in ("k", "g", "head"))
    plane_axes = ("head", "g")
    group = g_count * head_axis
    heads = H // group
    rows = queries.shape[0] * head_axis
    swap = [(0, 1), (1, 0)]

    def within_plane(x):
        return lax.all_to_all(x, plane_axes, split_axis=0, concat_axis=0, tiled=True)

    device = lax.axis_index(("k", "g", "core", "head")).astype(jnp.int32).reshape(1)
    packed_queries, own, far, mine, other = pack(
        group,
        g_count,
        head_axis,
        device,
        queries,
        query_tangent,
        key_rows,
        key_tangent,
        value_rows,
        value_tangent,
    )
    plane_queries = within_plane(packed_queries)
    pieces = join(mine, lax.ppermute(other, "core", swap))
    kv = [own]
    kv += [
        lax.ppermute(piece, ("g", "core", "head"), across_chips(turn, g_count, head_axis))
        for turn, piece in zip(TURNS, pieces)
    ]
    kv.append(lax.ppermute(far, ("g", "head"), [(i, i ^ FAR) for i in range(group)]))
    if k == 2:
        home_queries = [plane_queries[None], lax.ppermute(plane_queries, "k", swap)[None]]
    else:
        home_queries = [lax.all_gather(plane_queries, "k", axis=0, tiled=False)]
    away_queries = [lax.ppermute(q, "core", swap) for q in home_queries]

    width = out_weight.shape[1] // head_axis
    held = [hold(device, out_weight, head_axis, own)] if head_axis == 2 else []
    away, home = (
        attend(some, kv, device, k, g_count, head_axis, (held + kv)[0])
        for some in (away_queries, home_queries)
    )
    away, home = (some.reshape(k * g_count, rows, -1) for some in (away, home))
    count = k * g_count
    part_turns = PART_TURNS if count == len(PART_TURNS) else tuple(range(count))
    arrived = lax.ppermute(away, "core", swap)
    part_turns = part_turns[SPLIT:] + part_turns[:SPLIT]
    last, first = (
        merge_pair(device, home, arrived, heads, some, g_count, head_axis)
        for some in (part_turns[:-SPLIT], part_turns[-SPLIT:])
    )
    parts = last + first
    parts = [
        lax.ppermute(part, ("k", "g"), [(i, i ^ d) for i in range(count)]) if d else part
        for d, part in zip(part_turns, parts)
    ]

    merged = (2 * rows, out_weight.shape[0])
    merging = functools.partial(first_kernel, heads, g_count, head_axis, part_turns, len(held))
    if head_axis == 2:
        first = width // 2
        sent, both = project(
            merging, device, parts, out_weight, first, jnp.bfloat16, merged, held
        )
        received = [lax.ppermute(sent, "head", swap)]
        (sent,) = project(
            rest_kernel, device, [both], out_weight, width - first, jnp.bfloat16, None, held
        )
        received.append(lax.ppermute(sent, "head", swap))
        own_half = functools.partial(second_kernel, head_axis)
        (own,) = project(own_half, device, [both], out_weight, width, jnp.float32)
        outs = ()
        for part, arrived in enumerate(received):
            outs = sum_columns(own, arrived, part, outs)
        return tuple(outs)
    else:
        partial, _ = project(
            merging, device, parts, out_weight, width * head_axis, jnp.float32, merged
        )
        total = lax.psum_scatter(partial, "head", scatter_dimension=1, tiled=True)
    total = total.astype(jnp.bfloat16)
    return (total[:rows], total[rows:])


def solution(mesh):
    blk, head_axis = mesh.shape["blk"], mesh.shape["head"]
    g_count = math.gcd(H // head_axis, blk // 2)
    fine = Mesh(
        mesh.devices.reshape(blk // (2 * g_count), g_count, 2, head_axis),
        ("k", "g", "core", "head"),
    )
    rows = P(("k", "g", "core", "head"), None)
    return jax.shard_map(
        local,
        mesh=fine,
        in_specs=(rows,) * 6 + (P("head", None),),
        out_specs=(P(("k", "g", "core"), "head"),) * 2,
        check_vma=False,
    )
```
